32 devices in a mesh: gx: 8 (over y, x, core), yz: 4 (over z).
Axes of the slice: x: 2, y: 2, z: 4, core: 2. Of those that a mesh axis runs over, the one named last changes fastest.
Arguments:
- populations: bfloat16 [19, 128, 128, 128], P(None, 'gx', 'yz'), may hold values from -0.29882812 to 0.29882812
- levels: int32 [512], replicated, may hold values from 0 to 1
- refine_flags: int32 [512], replicated, may hold values from 0 to 2, as said below
- new_owner: int32 [512], replicated, may hold values from 0 to 31, as said below
Outputs:
- migrated: bfloat16 [768, 19, 4096], P(('gx', 'yz'))
The draws below stay inside these ranges and needn't reach their ends.
Inputs may be any that keep to these rules, and one draw needn't show every extreme that they name: On every device exactly 8 of the blocks it holds have refine_flags 1 or 2; all other blocks have 0. `new_owner`: A block with refine_flags 0 keeps the device that holds it. No device receives more than one flagged block from any one device, itself included. After migration a quarter of the devices hold exactly 24 blocks, a quarter exactly 16, and the rest exactly 16 minus half of 8.
All inputs are finite; a program needn't handle non-finite values.
Results may differ from the reference program's by a relative error of at most 0.0049.
Values may be sent and summed in bfloat16 or wider, within the bound.
A program may use at most 192 MiB of HBM per device.

```python
import jax
import jax.numpy as jnp
from jax import lax

BS = 16
HALF = 8
BX = 1
BY = 2
BZ = 8
MIG = 8
STEPS = 2
BLK = 16
CAP = 24
CX = 16
NX = 128
NY = 128
NZ = 128
NBLOCKS = 512
N_GX = 8
N_YZ = 4
DEVICES = 32


def migration_plan(key):
    plan_key = jax.random.fold_in(key, 17)
    key_rank, key_kind, key_load, key_source = jax.random.split(plan_key, 4)
    scores = jax.random.randint(key_rank, (DEVICES, BLK), 0, 1 << 20) * BLK + jnp.arange(BLK, dtype=jnp.int32)[None, :]
    block_ranks = jnp.argsort(jnp.argsort(scores, axis=1), axis=1).astype(jnp.int32)
    flag_kinds = 1 + jax.random.randint(key_kind, (DEVICES, BLK), 0, 2)
    flagged = block_ranks < MIG
    labels = jax.random.permutation(key_load, DEVICES).astype(jnp.int32)
    arrival_loads = jnp.where(labels < DEVICES // 4, 2 * MIG, jnp.where(labels < DEVICES // 2, MIG, MIG // 2))
    starts = jnp.cumsum(arrival_loads) - arrival_loads
    residues = jax.random.permutation(key_source, DEVICES).astype(jnp.int32)
    positions = residues[:, None] + block_ranks * DEVICES
    targets = jnp.sum((starts[None, None, :] <= positions[:, :, None]).astype(jnp.int32), axis=2) - 1
    owners = jnp.where(flagged, targets, jnp.arange(DEVICES, dtype=jnp.int32)[:, None])
    kind_map = jnp.where(flagged, flag_kinds, 0)

    def global_order(per_device):
        arranged = per_device.reshape(N_GX, N_YZ, BX, BY, BZ)
        return jnp.transpose(arranged, (0, 2, 1, 3, 4)).reshape(-1).astype(jnp.int32)
    return (global_order(kind_map), global_order(owners))


def draw_refine_flags(key, part):
    return migration_plan(key)[0]


def draw_new_owner(key, part):
    return migration_plan(key)[1]


def set_ends(drawn, stream_key, low, top_value):
    longest = drawn.shape.index(max(drawn.shape))
    spots = []
    for shift in (0, 1):
        where = [jax.random.randint(jax.random.fold_in(stream_key, axis), (), 0, length) for axis, length in enumerate(drawn.shape)]
        where[longest] = (where[longest] + shift) % drawn.shape[longest]
        spots.append(tuple(where))
    return drawn.at[spots[0]].set(low).at[spots[1]].set(top_value)


def block_scale(rng, shape, shards, low, high):
    gain, own = 1.0, jax.random.fold_in(rng, 6)
    for position, blocks in shards:
        draws = jnp.exp(jax.random.uniform(jax.random.fold_in(own, position), (blocks,), jnp.float32, low / len(shards), high / len(shards)))
        gain = gain * jnp.repeat(draws, shape[position] // blocks).reshape([-1 if axis == position else 1 for axis in range(len(shape))])
    return gain


def setup_inputs(seed: int = 0) -> dict:
    seeds = jax.random.split(jax.random.key(seed), 5)
    populations = jnp.clip(jax.random.uniform(seeds[0], (19, NX, NY, NZ), jnp.float32, -0.29882812, 0.29882812) * block_scale(seeds[0], (19, NX, NY, NZ), ((1, 8), (2, 4)), -0.4, 0.0), -0.29882812, 0.29882812).astype(jnp.bfloat16)
    levels = set_ends(jax.random.randint(seeds[1], (NBLOCKS,), 0, 2), jax.random.fold_in(seeds[1], 1), 0, 1).astype(jnp.int32)
    refine_flags = draw_refine_flags(jax.random.fold_in(seeds[4], 71), 0)
    new_owner = draw_new_owner(jax.random.fold_in(seeds[4], 71), 0)
    return dict(populations=populations, levels=levels, refine_flags=refine_flags, new_owner=new_owner)


VELOCITY_LIST = [[0, 0, 0], [1, 0, 0], [-1, 0, 0], [0, 1, 0], [0, -1, 0], [0, 0, 1], [0, 0, -1],
                 [1, 1, 0], [-1, -1, 0], [1, -1, 0], [-1, 1, 0], [1, 0, 1], [-1, 0, -1],
                 [1, 0, -1], [-1, 0, 1], [0, 1, 1], [0, -1, -1], [0, 1, -1], [0, -1, 1]]
WEIGHT_LIST = [1.0 / 3.0] + [1.0 / 18.0] * 6 + [1.0 / 36.0] * 12
OPPOSITE_LIST = [0, 2, 1, 4, 3, 6, 5, 8, 7, 10, 9, 12, 11, 14, 13, 16, 15, 18, 17]


def relax_rates(levels):
    return 1.0 / (0.5 + jnp.power(0.5, levels.astype(jnp.float32)))


def collide(current, relax_field):
    values = current.astype(jnp.float32)
    weights = jnp.asarray(WEIGHT_LIST, jnp.float32).reshape((19,) + (1,) * (values.ndim - 1))
    speeds = jnp.asarray(VELOCITY_LIST, jnp.float32)
    weighted = values * weights
    density = 1.0 + jnp.sum(weighted, axis=0)
    momentum = jnp.einsum("ic,i...->c...", speeds, weighted, precision=lax.Precision.HIGHEST)
    velocity = momentum / density
    speed_square = jnp.sum(velocity * velocity, axis=0)
    project = jnp.einsum("ic,c...->i...", speeds, velocity, precision=lax.Precision.HIGHEST)
    balance = density * (1.0 + 3.0 * project + 4.5 * project * project - 1.5 * speed_square) - 1.0
    return values - relax_field * (values - balance)


def propagate(collided):
    cells_pipe = collided.shape[1] - 2
    cells_cross = collided.shape[2] - 2
    interior = collided[:, 1:-1, 1:-1, :]
    results = []
    for direction in range(19):
        delta_first, delta_second, delta_third = VELOCITY_LIST[direction]
        shifted = collided[direction, 1 - delta_first:1 - delta_first + cells_pipe,
                           1 - delta_second:1 - delta_second + cells_cross, :]
        mirror = interior[OPPOSITE_LIST[direction]]
        if delta_third == 1:
            shifted = jnp.concatenate([mirror[:, :, :1], shifted[:, :, :-1]], axis=2)
        elif delta_third == -1:
            shifted = jnp.concatenate([shifted[:, :, 1:], mirror[:, :, -1:]], axis=2)
        results.append(shifted)
    return jnp.stack(results).astype(jnp.bfloat16)


def restrict(blocks):
    count = blocks.shape[0]
    values = blocks.astype(jnp.float32).reshape(count, 19, HALF, 2, HALF, 2, HALF, 2)
    return (jnp.sum(values, axis=(3, 5, 7)) * 0.125).reshape(count, 19, HALF * HALF * HALF).astype(jnp.bfloat16)


def prolong(coarse, flag_kinds):
    count = coarse.shape[0]
    fine_index = jnp.arange(BS, dtype=jnp.int32)
    parent = fine_index // 2
    neighbor_index = jnp.clip(jnp.where(fine_index % 2 == 0, parent - 1, parent + 1), 0, HALF - 1)
    coarse_index = jnp.arange(HALF, dtype=jnp.int32)
    inject = (parent[:, None] == coarse_index[None, :]).astype(jnp.float32)
    linear = 0.75 * inject + 0.25 * (neighbor_index[:, None] == coarse_index[None, :]).astype(jnp.float32)
    matrices = jnp.where((flag_kinds == 2)[:, None, None], linear[None], inject[None])
    values = coarse.astype(jnp.float32).reshape(count, 19, HALF, HALF, HALF)
    values = jnp.einsum("nah,nphij->npaij", matrices, values, precision=lax.Precision.HIGHEST)
    values = jnp.einsum("nbi,npaij->npabj", matrices, values, precision=lax.Precision.HIGHEST)
    values = jnp.einsum("ncj,npabj->npabc", matrices, values, precision=lax.Precision.HIGHEST)
    return values.reshape(count, 19, BS * BS * BS).astype(jnp.bfloat16)


def reference(populations, levels, refine_flags, new_owner):
    block_rates = relax_rates(levels).reshape(NX // BS, NY // BS, NZ // BS)
    relax_field = jnp.repeat(jnp.repeat(jnp.repeat(block_rates, BS, 0), BS, 1), BS, 2)
    padded_rates = jnp.pad(relax_field, ((1, 1), (1, 1), (0, 0)), mode="wrap")
    current = populations
    for sweep_number in range(STEPS):
        padded = jnp.pad(current, ((0, 0), (1, 1), (1, 1), (0, 0)), mode="wrap")

        def slab_step(offset):
            slab_piece = lax.dynamic_slice_in_dim(padded, offset, CX + 2, 1)
            rates_piece = lax.dynamic_slice_in_dim(padded_rates, offset, CX + 2, 0)
            return propagate(collide(slab_piece, rates_piece))

        slab_results = lax.map(slab_step, jnp.arange(N_GX, dtype=jnp.int32) * CX)
        current = jnp.transpose(slab_results, (1, 0, 2, 3, 4)).reshape(19, NX, NY, NZ)
    blocks = current.reshape(19, NX // BS, BS, NY // BS, BS, NZ // BS, BS)
    blocks = jnp.transpose(blocks, (1, 3, 5, 0, 2, 4, 6)).reshape(NBLOCKS, 19, BS * BS * BS)
    flagged_ids = jnp.nonzero(refine_flags != 0, size=MIG * DEVICES, fill_value=0)[0].astype(jnp.int32)

    def refine_group(block_ids):
        chosen = jnp.take(blocks, block_ids, axis=0)
        return prolong(restrict(chosen), jnp.take(refine_flags, block_ids))

    refined = lax.map(refine_group, flagged_ids.reshape(DEVICES, MIG)).reshape(DEVICES * MIG, 19, BS * BS * BS)
    blocks = blocks.at[flagged_ids].set(refined)
    block_pool = jnp.concatenate([blocks, jnp.zeros((1, 19, BS * BS * BS), jnp.bfloat16)], axis=0)

    def gather_owned(device):
        owned_ids = jnp.nonzero(new_owner == device, size=CAP, fill_value=NBLOCKS)[0].astype(jnp.int32)
        return jnp.take(block_pool, owned_ids, axis=0)

    migrated = lax.map(gather_owned, jnp.arange(DEVICES, dtype=jnp.int32))
    return migrated.reshape(DEVICES * CAP, 19, BS * BS * BS)
```

```python
import functools

import jax
import jax.numpy as jnp
import numpy as np
from jax import lax
from jax.experimental import pallas as pl
from jax.experimental.pallas import tpu as pltpu
from jax.sharding import PartitionSpec as P

BS = 16
HALF = 8
MIG = 8
CAP = 24
MESH = pl.DeviceIdType.MESH

VELOCITY = [
    (0, 0, 0),
    (1, 0, 0),
    (-1, 0, 0),
    (0, 1, 0),
    (0, -1, 0),
    (0, 0, 1),
    (0, 0, -1),
    (1, 1, 0),
    (-1, -1, 0),
    (1, -1, 0),
    (-1, 1, 0),
    (1, 0, 1),
    (-1, 0, -1),
    (1, 0, -1),
    (-1, 0, 1),
    (0, 1, 1),
    (0, -1, -1),
    (0, 1, -1),
    (0, -1, 1),
]
WEIGHT = [1.0 / 3.0] + [1.0 / 18.0] * 6 + [1.0 / 36.0] * 12
OPPOSITE = [0, 2, 1, 4, 3, 6, 5, 8, 7, 10, 9, 12, 11, 14, 13, 16, 15, 18, 17]
POPS = len(VELOCITY)
PAD = 8
FACES = [(1, 0), (-1, 0), (0, 1), (0, -1)]
CORNERS = [(1, 1), (-1, -1), (1, -1), (-1, 1)]
NEIGHBOURS = FACES + CORNERS
CROSSING = [
    [p for p in range(POPS) if VELOCITY[p][0] == 1],
    [p for p in range(POPS) if VELOCITY[p][0] == -1],
    [p for p in range(POPS) if VELOCITY[p][1] == 1],
    [p for p in range(POPS) if VELOCITY[p][1] == -1],
]


def total(terms):
    while len(terms) > 1:
        pairs = [a + b for a, b in zip(terms[::2], terms[1::2])]
        terms = pairs + ([terms[-1]] if len(terms) % 2 else [])
    return terms[0]


def collide(values, rate):
    edge = [values[p] for p in range(7, POPS)]
    density = 1.0 + (
        (1.0 / 3.0) * values[0] + (1.0 / 18.0) * total(values[1:7]) + (1.0 / 36.0) * total(edge)
    )
    inverse = 1.0 / density
    speeds = []
    for axis in range(3):
        face = None
        diagonal = None
        for p in range(1, POPS, 2):
            sign = VELOCITY[p][axis]
            if sign == 0:
                continue
            difference = values[p] - values[p + 1]
            if p < 7:
                face = difference if sign == 1 else -difference
            elif diagonal is None:
                diagonal = difference if sign == 1 else -difference
            else:
                diagonal = diagonal + difference if sign == 1 else diagonal - difference
        speeds.append(((1.0 / 18.0) * face + (1.0 / 36.0) * diagonal) * inverse)
    square = speeds[0] * speeds[0] + speeds[1] * speeds[1] + speeds[2] * speeds[2]
    keep = 1.0 - rate
    scaled = rate * density
    base = scaled * (1.0 - 1.5 * square) - rate
    results = [keep * values[0] + base]
    for p in range(1, POPS, 2):
        project = None
        for axis in range(3):
            sign = VELOCITY[p][axis]
            if sign == 0:
                continue
            if project is None:
                project = speeds[axis] if sign == 1 else -speeds[axis]
            else:
                project = project + speeds[axis] if sign == 1 else project - speeds[axis]
        even = base + scaled * (4.5 * project * project)
        odd = scaled * (3.0 * project)
        results.append(keep * values[p] + (even + odd))
        results.append(keep * values[p + 1] + (even - odd))
    return results


def steps_kernel(
    nx,
    ny,
    pop_ref,
    rate_ref,
    out_ref,
    first,
    second,
    x_send,
    x_recv,
    y_send,
    y_recv,
    c_send,
    c_recv,
    send_sem,
    recv_sem,
):
    nz = pop_ref.shape[3]
    gx = lax.axis_index("gx")
    yz = lax.axis_index("yz")
    gx_count = lax.axis_size("gx")
    yz_count = lax.axis_size("yz")

    def device(offset):
        return (
            lax.rem(gx + offset[0] + gx_count, gx_count),
            lax.rem(yz + offset[1] + yz_count, yz_count),
        )

    barrier = pltpu.get_barrier_semaphore()
    for offset in NEIGHBOURS:
        pl.semaphore_signal(barrier, inc=1, device_id=device(offset), device_id_type=MESH)
    lane = lax.broadcasted_iota(jnp.int32, (BS, nz), 1)

    def put(target, x, start, collided):
        for p in range(POPS):
            rounded = collided[p].astype(jnp.bfloat16).astype(jnp.float32)
            target[p, x + 1, PAD + start : PAD + start + BS, :] = rounded

    def gather(source, x, start):
        values = []
        for p in range(POPS):
            dx, dy, dz = VELOCITY[p]
            low = PAD + start - dy
            value = source[p, x + 1 - dx, low : low + BS, :]
            if dz != 0:
                mirror = source[OPPOSITE[p], x + 1, PAD + start : PAD + start + BS, :]
                if dz == 1:
                    value = jnp.where(lane == 0, mirror, pltpu.roll(value, 1, axis=1))
                else:
                    value = jnp.where(lane == nz - 1, mirror, pltpu.roll(value, nz - 1, axis=1))
            values.append(value)
        return values

    def exchange(step, field):
        for side in range(2):
            plane = nx if side == 0 else 1
            row = PAD + ny - 1 if side == 0 else PAD
            for k, p in enumerate(CROSSING[side]):
                x_send[step, side, k] = field[p, plane, PAD : PAD + ny, :]

        def pack(x, carry):
            for side in range(2):
                row = PAD + ny - 1 if side == 0 else PAD
                for k, p in enumerate(CROSSING[2 + side]):
                    y_send[step, side, k, pl.ds(x, 1), :] = field[p, x + 1, row : row + 1, :]
            return carry

        lax.fori_loop(0, nx, pack, 0)
        for c, (dx, dy) in enumerate(CORNERS):
            low = ny if dy == 1 else PAD
            c_send[step, c] = field[7 + c, nx if dx == 1 else 1, low : low + PAD, :]
        if step == 0:
            pl.semaphore_wait(barrier, len(NEIGHBOURS))
        copies = []
        for n, offset in enumerate(NEIGHBOURS):
            if n < 2:
                pair = (x_send.at[step, n], x_recv.at[step, n])
            elif n < 4:
                pair = (y_send.at[step, n - 2], y_recv.at[step, n - 2])
            else:
                pair = (c_send.at[step, n - 4], c_recv.at[step, n - 4])
            copy = pltpu.make_async_remote_copy(
                src_ref=pair[0],
                dst_ref=pair[1],
                send_sem=send_sem.at[step, n],
                recv_sem=recv_sem.at[step, n],
                device_id=device(offset),
                device_id_type=MESH,
            )
            copy.start()
            copies.append(copy)
        for copy in copies:
            copy.wait()
        for side in range(2):
            for k, p in enumerate(CROSSING[side]):
                field[p, 0 if side == 0 else nx + 1, PAD : PAD + ny, :] = x_recv[step, side, k]

        def unpack(x, carry):
            for side in range(2):
                row = PAD - 1 if side == 0 else PAD + ny
                for k, p in enumerate(CROSSING[2 + side]):
                    field[p, x + 1, row : row + 1, :] = y_recv[step, side, k, pl.ds(x, 1), :]
            return carry

        lax.fori_loop(0, nx, unpack, 0)
        for c, (dx, dy) in enumerate(CORNERS):
            low = 0 if dy == 1 else PAD + ny
            field[7 + c, 0 if dx == 1 else nx + 1, low : low + PAD, :] = c_recv[step, c]

    starts = range(0, ny, BS)

    def begin(x, carry):
        for start in starts:
            values = [pop_ref[p, x, start : start + BS, :].astype(jnp.float32) for p in range(POPS)]
            put(first, x, start, collide(values, rate_ref[start : start + BS, :]))
        return carry

    def middle(x, carry):
        for start in starts:
            values = gather(first, x, start)
            put(second, x, start, collide(values, rate_ref[start : start + BS, :]))
        return carry

    def finish(x, carry):
        for start in starts:
            values = gather(second, x, start)
            for p in range(POPS):
                out_ref[p, x, start : start + BS, :] = values[p].astype(jnp.bfloat16)
        return carry

    lax.fori_loop(0, nx, begin, 0)
    exchange(0, first)
    lax.fori_loop(0, nx, middle, 0)
    exchange(1, second)
    lax.fori_loop(0, nx, finish, 0)


def run_steps(populations, rates):
    _, nx, ny, nz = populations.shape
    field = pltpu.VMEM((POPS, nx + 2, ny + 2 * PAD, nz), jnp.float32)
    x_face = pltpu.VMEM((2, 2, 5, ny, nz), jnp.float32)
    y_face = pltpu.VMEM((2, 2, 5, nx, nz), jnp.float32)
    corner = pltpu.VMEM((2, 4, PAD, nz), jnp.float32)
    return pl.pallas_call(
        functools.partial(steps_kernel, nx, ny),
        out_shape=jax.ShapeDtypeStruct(populations.shape, jnp.bfloat16),
        in_specs=[pl.BlockSpec(memory_space=pltpu.VMEM)] * 2,
        out_specs=pl.BlockSpec(memory_space=pltpu.VMEM),
        scratch_shapes=[
            field,
            field,
            x_face,
            x_face,
            y_face,
            y_face,
            corner,
            corner,
            pltpu.SemaphoreType.DMA((2, len(NEIGHBOURS))),
            pltpu.SemaphoreType.DMA((2, len(NEIGHBOURS))),
        ],
        compiler_params=pltpu.CompilerParams(
            collective_id=0, has_side_effects=True, vmem_limit_bytes=48 * 2**20
        ),
        name="steps",
    )(populations, rates)


ROWS = 32
CHUNK = 4


def layout_kernel(nx, ny, nz, state_ref, select_ref, pool_ref, fine, packed):
    eighths = ny // 8
    across = nz // BS
    fine[...] = jnp.zeros_like(fine)

    def part(c, carry):
        for inner in range(CHUNK):
            x = c * CHUNK + inner
            for p in range(POPS):
                fine[p * ny : (p + 1) * ny, :] = state_ref[p, x].astype(jnp.float32)
            for e in range(eighths):
                row = (inner * eighths + e) * ROWS
                for j in range(8):
                    rows = fine[pl.ds(e * 8 + j, ROWS, stride=ny), :]
                    packed[row : row + ROWS, j * nz : (j + 1) * nz] = rows.astype(jnp.bfloat16)
        result = jnp.dot(packed[...], select_ref[...], preferred_element_type=jnp.float32)
        result = result.astype(jnp.bfloat16)
        for inner in range(CHUNK):
            for e in range(eighths):
                row = (inner * eighths + e) * ROWS
                lanes = pl.ds(pl.multiple_of((c * CHUNK * 2 + inner * 2 + e % 2) * 128, 128), 128)
                for k in range(across):
                    pool_ref[e // 2 * across + k, :, lanes] = result[
                        row : row + POPS, k * 128 : (k + 1) * 128
                    ]
        return carry

    lax.fori_loop(0, nx // CHUNK, part, 0)


def lay_out(state):
    _, nx, ny, nz = state.shape
    across = nz // BS
    select = np.zeros((8 * nz, across * 128), np.float32)
    for j in range(8):
        for z in range(nz):
            select[j * nz + z, z // BS * 128 + j * BS + z % BS] = 1.0
    blocks = ny // BS * across
    return pl.pallas_call(
        functools.partial(layout_kernel, nx, ny, nz),
        out_shape=jax.ShapeDtypeStruct((blocks, POPS, BS**3), jnp.bfloat16),
        in_specs=[pl.BlockSpec(memory_space=pltpu.VMEM)] * 2,
        out_specs=pl.BlockSpec(memory_space=pltpu.VMEM),
        scratch_shapes=[
            pltpu.VMEM((ROWS * ny, nz), jnp.float32),
            pltpu.VMEM((CHUNK * (ny // 8) * ROWS, 8 * nz), jnp.bfloat16),
        ],
        compiler_params=pltpu.CompilerParams(vmem_limit_bytes=48 * 2**20),
        name="layout",
    )(state, jnp.asarray(select, jnp.bfloat16))


def fill_kernel(source_ref, pool_ref, arrival_ref, empty_ref, out_ref, sem):
    blocks = pool_ref.shape[0]
    arrivals = arrival_ref.shape[0]

    def begin(slot, carry):
        source = source_ref[slot]

        @pl.when(source < blocks)
        def _():
            index = jnp.minimum(source, blocks - 1)
            pltpu.make_async_copy(pool_ref.at[index], out_ref.at[slot], sem.at[slot]).start()

        @pl.when((source >= blocks) & (source < blocks + arrivals))
        def _():
            index = jnp.clip(source - blocks, 0, arrivals - 1)
            pltpu.make_async_copy(arrival_ref.at[index], out_ref.at[slot], sem.at[slot]).start()

        @pl.when(source >= blocks + arrivals)
        def _():
            pltpu.make_async_copy(empty_ref, out_ref.at[slot], sem.at[slot]).start()

        return carry

    def end(slot, carry):
        pltpu.make_async_copy(empty_ref, out_ref.at[slot], sem.at[slot]).wait()
        return carry

    lax.fori_loop(0, CAP, begin, 0)
    lax.fori_loop(0, CAP, end, 0)


def fill(source, pool, arrivals):
    empty = jnp.zeros(pool.shape[1:], jnp.bfloat16)
    return pl.pallas_call(
        fill_kernel,
        out_shape=jax.ShapeDtypeStruct((CAP,) + pool.shape[1:], jnp.bfloat16),
        in_specs=[pl.BlockSpec(memory_space=pltpu.SMEM)] + [pl.BlockSpec(memory_space=pl.ANY)] * 3,
        out_specs=pl.BlockSpec(memory_space=pl.ANY),
        scratch_shapes=[pltpu.SemaphoreType.DMA((CAP,))],
        name="fill",
    )(source, pool, arrivals, empty)


def transfer_matrices():
    parent = np.arange(BS) // 2
    step = np.where(np.arange(BS) % 2 == 0, -1, 1)
    neighbour = np.clip(parent + step, 0, HALF - 1)
    inject = (parent[:, None] == np.arange(HALF)[None, :]).astype(np.float32)
    linear = 0.75 * inject + 0.25 * (neighbour[:, None] == np.arange(HALF)[None, :])

    def cube(matrix):
        return np.kron(np.kron(matrix, matrix), matrix)

    merge = cube(inject) * 0.125
    spread = np.concatenate([cube(inject).T, cube(linear).T], axis=0)
    return merge, spread


def body(populations, levels, refine_flags, new_owner):
    slab_count = lax.axis_size("gx")
    column_count = lax.axis_size("yz")
    slab = lax.axis_index("gx")
    column = lax.axis_index("yz")
    me = slab * column_count + column
    devices = slab_count * column_count
    _, nx, ny, nz = populations.shape
    across = nz // BS
    rows = ny // BS
    local = rows * across
    base = me * local
    block_total = new_owner.shape[0]

    local_levels = lax.dynamic_slice(levels, (base,), (local,)).reshape(rows, across)
    block_rates = 1.0 / (0.5 + jnp.power(0.5, local_levels.astype(jnp.float32)))
    rates = jnp.repeat(jnp.repeat(block_rates, BS, 0), BS, 1)

    ids = jnp.arange(block_total, dtype=jnp.int32)
    owned = new_owner == me
    before = owned[None, :] & (ids[None, :] < ids[:, None])
    rank = jnp.sum(before.astype(jnp.int32), axis=1)
    slots = jnp.arange(CAP, dtype=jnp.int32)
    hit = owned[None, :] & (rank[None, :] == slots[:, None])
    slot_id = jnp.sum(jnp.where(hit, ids[None, :], 0), axis=1)
    slot_kind = jnp.sum(jnp.where(hit, refine_flags[None, :], 0), axis=1)
    slot_used = jnp.any(hit, axis=1)
    flagged = slot_kind != 0
    slot_rank = jnp.sum(
        (flagged[None, :] & (slots[None, :] < slots[:, None])).astype(jnp.int32), axis=1
    )
    order = jnp.arange(2 * MIG, dtype=jnp.int32)
    match = flagged[None, :] & (slot_rank[None, :] == order[:, None])
    arrival_id = jnp.sum(jnp.where(match, slot_id[None, :], 0), axis=1)
    arrival_kind = jnp.sum(jnp.where(match, slot_kind[None, :], 0), axis=1)
    source = jnp.where(
        slot_used,
        jnp.where(flagged, local + slot_rank, slot_id % local),
        local + 2 * MIG,
    )

    local_flags = lax.dynamic_slice(refine_flags, (base,), (local,))
    local_owner = lax.dynamic_slice(new_owner, (base,), (local,))
    leaving = (local_flags != 0)[None, :] & (
        local_owner[None, :] == jnp.arange(devices, dtype=jnp.int32)[:, None]
    )
    leaving_block = jnp.sum(
        jnp.where(leaving, jnp.arange(local, dtype=jnp.int32)[None, :], 0), axis=1
    )

    state = run_steps(populations, rates)
    pool = lay_out(state)
    merge, spread = transfer_matrices()
    coarse = jnp.einsum(
        "bpf,fc->bpc",
        pool,
        jnp.asarray(merge, jnp.bfloat16),
        preferred_element_type=jnp.float32,
    ).astype(jnp.bfloat16)
    outgoing = jnp.take(coarse, leaving_block, axis=0)
    incoming = lax.all_to_all(outgoing, ("gx", "yz"), split_axis=0, concat_axis=0, tiled=True)
    arrived = jnp.take(incoming, arrival_id // local, axis=0)
    zero = jnp.zeros((), jnp.bfloat16)
    kinds = arrival_kind[:, None, None]
    both = jnp.concatenate(
        [jnp.where(kinds == 1, arrived, zero), jnp.where(kinds == 2, arrived, zero)], axis=2
    )
    refined = jnp.einsum(
        "bpc,cf->bpf",
        both,
        jnp.asarray(spread, jnp.bfloat16),
        preferred_element_type=jnp.float32,
    ).astype(jnp.bfloat16)
    return fill(source, pool, refined)


def solution(mesh):
    placed = (P(None, "gx", "yz", None), P(), P(), P())
    return jax.shard_map(
        body, mesh=mesh, in_specs=placed, out_specs=P(("gx", "yz"), None, None), check_vma=False
    )
```

```python
import functools

import jax
import jax.numpy as jnp
import numpy as np
from jax import lax
from jax.experimental import pallas as pl
from jax.experimental.pallas import tpu as pltpu
from jax.sharding import PartitionSpec as P

BS = 16
HALF = 8
MIG = 8
CAP = 24
MESH = pl.DeviceIdType.MESH

VELOCITY = [
    (0, 0, 0),
    (1, 0, 0),
    (-1, 0, 0),
    (0, 1, 0),
    (0, -1, 0),
    (0, 0, 1),
    (0, 0, -1),
    (1, 1, 0),
    (-1, -1, 0),
    (1, -1, 0),
    (-1, 1, 0),
    (1, 0, 1),
    (-1, 0, -1),
    (1, 0, -1),
    (-1, 0, 1),
    (0, 1, 1),
    (0, -1, -1),
    (0, 1, -1),
    (0, -1, 1),
]
WEIGHT = [1.0 / 3.0] + [1.0 / 18.0] * 6 + [1.0 / 36.0] * 12
OPPOSITE = [0, 2, 1, 4, 3, 6, 5, 8, 7, 10, 9, 12, 11, 14, 13, 16, 15, 18, 17]
POPS = len(VELOCITY)
PAD = 8
FACES = [(1, 0), (-1, 0), (0, 1), (0, -1)]
CORNERS = [(1, 1), (-1, -1), (1, -1), (-1, 1)]
NEIGHBOURS = FACES + CORNERS
CROSSING = [
    [p for p in range(POPS) if VELOCITY[p][0] == 1],
    [p for p in range(POPS) if VELOCITY[p][0] == -1],
    [p for p in range(POPS) if VELOCITY[p][1] == 1],
    [p for p in range(POPS) if VELOCITY[p][1] == -1],
]


def total(terms):
    while len(terms) > 1:
        pairs = [a + b for a, b in zip(terms[::2], terms[1::2])]
        terms = pairs + ([terms[-1]] if len(terms) % 2 else [])
    return terms[0]


def collide(values, rate):
    edge = [values[p] for p in range(7, POPS)]
    density = 1.0 + (
        (1.0 / 3.0) * values[0] + (1.0 / 18.0) * total(values[1:7]) + (1.0 / 36.0) * total(edge)
    )
    inverse = 1.0 / density
    speeds = []
    for axis in range(3):
        face = None
        diagonal = None
        for p in range(1, POPS, 2):
            sign = VELOCITY[p][axis]
            if sign == 0:
                continue
            difference = values[p] - values[p + 1]
            if p < 7:
                face = difference if sign == 1 else -difference
            elif diagonal is None:
                diagonal = difference if sign == 1 else -difference
            else:
                diagonal = diagonal + difference if sign == 1 else diagonal - difference
        speeds.append(((1.0 / 18.0) * face + (1.0 / 36.0) * diagonal) * inverse)
    square = speeds[0] * speeds[0] + speeds[1] * speeds[1] + speeds[2] * speeds[2]
    keep = 1.0 - rate
    scaled = rate * density
    base = scaled * (1.0 - 1.5 * square) - rate
    results = [keep * values[0] + base]
    for p in range(1, POPS, 2):
        project = None
        for axis in range(3):
            sign = VELOCITY[p][axis]
            if sign == 0:
                continue
            if project is None:
                project = speeds[axis] if sign == 1 else -speeds[axis]
            else:
                project = project + speeds[axis] if sign == 1 else project - speeds[axis]
        even = base + scaled * (4.5 * project * project)
        odd = scaled * (3.0 * project)
        results.append(keep * values[p] + (even + odd))
        results.append(keep * values[p + 1] + (even - odd))
    return results


def steps_kernel(
    nx,
    ny,
    pop_ref,
    rate_ref,
    out_ref,
    first,
    second,
    x_send,
    x_recv,
    y_send,
    y_recv,
    c_send,
    c_recv,
    send_sem,
    recv_sem,
):
    nz = pop_ref.shape[3]
    gx = lax.axis_index("gx")
    yz = lax.axis_index("yz")
    gx_count = lax.axis_size("gx")
    yz_count = lax.axis_size("yz")

    def device(offset):
        return (
            lax.rem(gx + offset[0] + gx_count, gx_count),
            lax.rem(yz + offset[1] + yz_count, yz_count),
        )

    barrier = pltpu.get_barrier_semaphore()
    for offset in NEIGHBOURS:
        pl.semaphore_signal(barrier, inc=1, device_id=device(offset), device_id_type=MESH)
    lane = lax.broadcasted_iota(jnp.int32, (BS, nz), 1)

    def put(target, x, start, collided):
        for p in range(POPS):
            rounded = collided[p].astype(jnp.bfloat16).astype(jnp.float32)
            target[p, x + 1, PAD + start : PAD + start + BS, :] = rounded

    def gather(source, x, start):
        values = []
        for p in range(POPS):
            dx, dy, dz = VELOCITY[p]
            low = PAD + start - dy
            value = source[p, x + 1 - dx, low : low + BS, :]
            if dz != 0:
                mirror = source[OPPOSITE[p], x + 1, PAD + start : PAD + start + BS, :]
                if dz == 1:
                    value = jnp.where(lane == 0, mirror, pltpu.roll(value, 1, axis=1))
                else:
                    value = jnp.where(lane == nz - 1, mirror, pltpu.roll(value, nz - 1, axis=1))
            values.append(value)
        return values

    def exchange(step, field):
        for side in range(2):
            plane = nx if side == 0 else 1
            row = PAD + ny - 1 if side == 0 else PAD
            for k, p in enumerate(CROSSING[side]):
                x_send[step, side, k] = field[p, plane, PAD : PAD + ny, :]

        def pack(x, carry):
            for side in range(2):
                row = PAD + ny - 1 if side == 0 else PAD
                for k, p in enumerate(CROSSING[2 + side]):
                    y_send[step, side, k, pl.ds(x, 1), :] = field[p, x + 1, row : row + 1, :]
            return carry

        lax.fori_loop(0, nx, pack, 0)
        for c, (dx, dy) in enumerate(CORNERS):
            low = ny if dy == 1 else PAD
            c_send[step, c] = field[7 + c, nx if dx == 1 else 1, low : low + PAD, :]
        if step == 0:
            pl.semaphore_wait(barrier, len(NEIGHBOURS))
        copies = []
        for n, offset in enumerate(NEIGHBOURS):
            if n < 2:
                pair = (x_send.at[step, n], x_recv.at[step, n])
            elif n < 4:
                pair = (y_send.at[step, n - 2], y_recv.at[step, n - 2])
            else:
                pair = (c_send.at[step, n - 4], c_recv.at[step, n - 4])
            copy = pltpu.make_async_remote_copy(
                src_ref=pair[0],
                dst_ref=pair[1],
                send_sem=send_sem.at[step, n],
                recv_sem=recv_sem.at[step, n],
                device_id=device(offset),
                device_id_type=MESH,
            )
            copy.start()
            copies.append(copy)
        for copy in copies:
            copy.wait()
        for side in range(2):
            for k, p in enumerate(CROSSING[side]):
                field[p, 0 if side == 0 else nx + 1, PAD : PAD + ny, :] = x_recv[step, side, k]

        def unpack(x, carry):
            for side in range(2):
                row = PAD - 1 if side == 0 else PAD + ny
                for k, p in enumerate(CROSSING[2 + side]):
                    field[p, x + 1, row : row + 1, :] = y_recv[step, side, k, pl.ds(x, 1), :]
            return carry

        lax.fori_loop(0, nx, unpack, 0)
        for c, (dx, dy) in enumerate(CORNERS):
            low = 0 if dy == 1 else PAD + ny
            field[7 + c, 0 if dx == 1 else nx + 1, low : low + PAD, :] = c_recv[step, c]

    starts = range(0, ny, BS)

    def begin(x, carry):
        for start in starts:
            values = [pop_ref[p, x, start : start + BS, :].astype(jnp.float32) for p in range(POPS)]
            put(first, x, start, collide(values, rate_ref[start : start + BS, :]))
        return carry

    def middle(x, carry):
        for start in starts:
            values = gather(first, x, start)
            put(second, x, start, collide(values, rate_ref[start : start + BS, :]))
        return carry

    def finish(x, carry):
        for start in starts:
            values = gather(second, x, start)
            for p in range(POPS):
                out_ref[p, x, start : start + BS, :] = values[p].astype(jnp.bfloat16)
        return carry

    lax.fori_loop(0, nx, begin, 0)
    exchange(0, first)
    lax.fori_loop(0, nx, middle, 0)
    exchange(1, second)
    lax.fori_loop(0, nx, finish, 0)


def run_steps(populations, rates):
    _, nx, ny, nz = populations.shape
    field = pltpu.VMEM((POPS, nx + 2, ny + 2 * PAD, nz), jnp.float32)
    x_face = pltpu.VMEM((2, 2, 5, ny, nz), jnp.float32)
    y_face = pltpu.VMEM((2, 2, 5, nx, nz), jnp.float32)
    corner = pltpu.VMEM((2, 4, PAD, nz), jnp.float32)
    return pl.pallas_call(
        functools.partial(steps_kernel, nx, ny),
        out_shape=jax.ShapeDtypeStruct(populations.shape, jnp.bfloat16),
        in_specs=[pl.BlockSpec(memory_space=pltpu.VMEM)] * 2,
        out_specs=pl.BlockSpec(memory_space=pltpu.VMEM),
        scratch_shapes=[
            field,
            field,
            x_face,
            x_face,
            y_face,
            y_face,
            corner,
            corner,
            pltpu.SemaphoreType.DMA((2, len(NEIGHBOURS))),
            pltpu.SemaphoreType.DMA((2, len(NEIGHBOURS))),
        ],
        compiler_params=pltpu.CompilerParams(
            collective_id=0, has_side_effects=True, vmem_limit_bytes=48 * 2**20
        ),
        name="steps",
    )(populations, rates)


ROWS = 32
CHUNK = 4


def layout_kernel(nx, ny, nz, state_ref, select_ref, pool_ref, fine, packed):
    eighths = ny // 8
    across = nz // BS
    fine[...] = jnp.zeros_like(fine)

    def part(c, carry):
        for inner in range(CHUNK):
            x = c * CHUNK + inner
            for p in range(POPS):
                fine[p * ny : (p + 1) * ny, :] = state_ref[p, x].astype(jnp.float32)
            for e in range(eighths):
                row = (inner * eighths + e) * ROWS
                for j in range(8):
                    rows = fine[pl.ds(e * 8 + j, ROWS, stride=ny), :]
                    packed[row : row + ROWS, j * nz : (j + 1) * nz] = rows.astype(jnp.bfloat16)
        result = jnp.dot(packed[...], select_ref[...], preferred_element_type=jnp.float32)
        result = result.astype(jnp.bfloat16)
        for inner in range(CHUNK):
            for e in range(eighths):
                row = (inner * eighths + e) * ROWS
                lanes = pl.ds(pl.multiple_of((c * CHUNK * 2 + inner * 2 + e % 2) * 128, 128), 128)
                for k in range(across):
                    pool_ref[e // 2 * across + k, :, lanes] = result[
                        row : row + POPS, k * 128 : (k + 1) * 128
                    ]
        return carry

    lax.fori_loop(0, nx // CHUNK, part, 0)


def lay_out(state):
    _, nx, ny, nz = state.shape
    across = nz // BS
    select = np.zeros((8 * nz, across * 128), np.float32)
    for j in range(8):
        for z in range(nz):
            select[j * nz + z, z // BS * 128 + j * BS + z % BS] = 1.0
    blocks = ny // BS * across
    return pl.pallas_call(
        functools.partial(layout_kernel, nx, ny, nz),
        out_shape=jax.ShapeDtypeStruct((blocks, POPS, BS**3), jnp.bfloat16),
        in_specs=[pl.BlockSpec(memory_space=pltpu.VMEM)] * 2,
        out_specs=pl.BlockSpec(memory_space=pltpu.VMEM),
        scratch_shapes=[
            pltpu.VMEM((ROWS * ny, nz), jnp.float32),
            pltpu.VMEM((CHUNK * (ny // 8) * ROWS, 8 * nz), jnp.bfloat16),
        ],
        compiler_params=pltpu.CompilerParams(vmem_limit_bytes=48 * 2**20),
        name="layout",
    )(state, jnp.asarray(select, jnp.bfloat16))


def fill_kernel(source_ref, pool_ref, arrival_ref, out_ref, held):
    blocks = pool_ref.shape[0]
    arrivals = arrival_ref.shape[0]

    def place(slot, carry):
        source = source_ref[slot]
        rows = pl.ds(slot, POPS, stride=CAP)

        @pl.when(source < blocks)
        def _():
            value = pool_ref[jnp.minimum(source, blocks - 1)].astype(jnp.float32)
            for k in range(LANES):
                held[k, rows, :] = value[:, k * 128 : (k + 1) * 128]

        @pl.when((source >= blocks) & (source < blocks + arrivals))
        def _():
            index = jnp.clip(source - blocks, 0, arrivals - 1)
            value = arrival_ref[index].astype(jnp.float32)
            for k in range(LANES):
                held[k, rows, :] = value[:, k * 128 : (k + 1) * 128]

        @pl.when(source >= blocks + arrivals)
        def _():
            for k in range(LANES):
                held[k, rows, :] = jnp.zeros((POPS, 128), jnp.float32)

        return carry

    lax.fori_loop(0, CAP, place, 0)

    def emit(p, carry):
        rows = pl.ds(pl.multiple_of(p * CAP, 8), CAP)
        for k in range(LANES):
            out_ref[p, :, k * 128 : (k + 1) * 128] = held[k, rows, :].astype(jnp.bfloat16)
        return carry

    lax.fori_loop(0, POPS, emit, 0)


LANES = BS**3 // 128


def fill(source, pool, arrivals):
    slotted = pl.pallas_call(
        fill_kernel,
        out_shape=jax.ShapeDtypeStruct((POPS, CAP, BS**3), jnp.bfloat16),
        in_specs=[pl.BlockSpec(memory_space=pltpu.SMEM)]
        + [pl.BlockSpec(memory_space=pltpu.VMEM)] * 2,
        out_specs=pl.BlockSpec(memory_space=pltpu.VMEM),
        scratch_shapes=[pltpu.VMEM((LANES, POPS * CAP, 128), jnp.float32)],
        compiler_params=pltpu.CompilerParams(vmem_limit_bytes=48 * 2**20),
        name="fill",
    )(source, pool, arrivals)
    return jnp.transpose(slotted, (1, 0, 2))


def transfer_matrices():
    parent = np.arange(BS) // 2
    step = np.where(np.arange(BS) % 2 == 0, -1, 1)
    neighbour = np.clip(parent + step, 0, HALF - 1)
    inject = (parent[:, None] == np.arange(HALF)[None, :]).astype(np.float32)
    linear = 0.75 * inject + 0.25 * (neighbour[:, None] == np.arange(HALF)[None, :])

    def cube(matrix):
        return np.kron(np.kron(matrix, matrix), matrix)

    merge = cube(inject) * 0.125
    spread = np.concatenate([cube(inject).T, cube(linear).T], axis=0)
    return merge, spread


def body(populations, levels, refine_flags, new_owner):
    slab_count = lax.axis_size("gx")
    column_count = lax.axis_size("yz")
    slab = lax.axis_index("gx")
    column = lax.axis_index("yz")
    me = slab * column_count + column
    devices = slab_count * column_count
    _, nx, ny, nz = populations.shape
    across = nz // BS
    rows = ny // BS
    local = rows * across
    base = me * local
    block_total = new_owner.shape[0]

    local_levels = lax.dynamic_slice(levels, (base,), (local,)).reshape(rows, across)
    block_rates = 1.0 / (0.5 + jnp.power(0.5, local_levels.astype(jnp.float32)))
    rates = jnp.repeat(jnp.repeat(block_rates, BS, 0), BS, 1)

    ids = jnp.arange(block_total, dtype=jnp.int32)
    owned = new_owner == me
    before = owned[None, :] & (ids[None, :] < ids[:, None])
    rank = jnp.sum(before.astype(jnp.int32), axis=1)
    slots = jnp.arange(CAP, dtype=jnp.int32)
    hit = owned[None, :] & (rank[None, :] == slots[:, None])
    slot_id = jnp.sum(jnp.where(hit, ids[None, :], 0), axis=1)
    slot_kind = jnp.sum(jnp.where(hit, refine_flags[None, :], 0), axis=1)
    slot_used = jnp.any(hit, axis=1)
    flagged = slot_kind != 0
    slot_rank = jnp.sum(
        (flagged[None, :] & (slots[None, :] < slots[:, None])).astype(jnp.int32), axis=1
    )
    order = jnp.arange(2 * MIG, dtype=jnp.int32)
    match = flagged[None, :] & (slot_rank[None, :] == order[:, None])
    arrival_id = jnp.sum(jnp.where(match, slot_id[None, :], 0), axis=1)
    arrival_kind = jnp.sum(jnp.where(match, slot_kind[None, :], 0), axis=1)
    source = jnp.where(
        slot_used,
        jnp.where(flagged, local + slot_rank, slot_id % local),
        local + 2 * MIG,
    )

    local_flags = lax.dynamic_slice(refine_flags, (base,), (local,))
    local_owner = lax.dynamic_slice(new_owner, (base,), (local,))
    leaving = (local_flags != 0)[None, :] & (
        local_owner[None, :] == jnp.arange(devices, dtype=jnp.int32)[:, None]
    )
    leaving_block = jnp.sum(
        jnp.where(leaving, jnp.arange(local, dtype=jnp.int32)[None, :], 0), axis=1
    )

    state = run_steps(populations, rates)
    pool = lay_out(state)
    merge, spread = transfer_matrices()
    coarse = jnp.einsum(
        "bpf,fc->bpc",
        pool,
        jnp.asarray(merge, jnp.bfloat16),
        preferred_element_type=jnp.float32,
    ).astype(jnp.bfloat16)
    outgoing = jnp.take(coarse, leaving_block, axis=0)
    incoming = lax.all_to_all(outgoing, ("gx", "yz"), split_axis=0, concat_axis=0, tiled=True)
    arrived = jnp.take(incoming, arrival_id // local, axis=0)
    zero = jnp.zeros((), jnp.bfloat16)
    kinds = arrival_kind[:, None, None]
    both = jnp.concatenate(
        [jnp.where(kinds == 1, arrived, zero), jnp.where(kinds == 2, arrived, zero)], axis=2
    )
    refined = jnp.einsum(
        "bpc,cf->bpf",
        both,
        jnp.asarray(spread, jnp.bfloat16),
        preferred_element_type=jnp.float32,
    ).astype(jnp.bfloat16)
    return fill(source, pool, refined)


def solution(mesh):
    placed = (P(None, "gx", "yz", None), P(), P(), P())
    return jax.shard_map(
        body, mesh=mesh, in_specs=placed, out_specs=P(("gx", "yz"), None, None), check_vma=False
    )
```

```python
import functools

import jax
import jax.numpy as jnp
import numpy as np
from jax import lax
from jax.experimental import pallas as pl
from jax.experimental.pallas import tpu as pltpu
from jax.sharding import PartitionSpec as P

BS = 16
HALF = 8
MIG = 8
CAP = 24
MESH = pl.DeviceIdType.MESH

VELOCITY = [
    (0, 0, 0),
    (1, 0, 0),
    (-1, 0, 0),
    (0, 1, 0),
    (0, -1, 0),
    (0, 0, 1),
    (0, 0, -1),
    (1, 1, 0),
    (-1, -1, 0),
    (1, -1, 0),
    (-1, 1, 0),
    (1, 0, 1),
    (-1, 0, -1),
    (1, 0, -1),
    (-1, 0, 1),
    (0, 1, 1),
    (0, -1, -1),
    (0, 1, -1),
    (0, -1, 1),
]
WEIGHT = [1.0 / 3.0] + [1.0 / 18.0] * 6 + [1.0 / 36.0] * 12
OPPOSITE = [0, 2, 1, 4, 3, 6, 5, 8, 7, 10, 9, 12, 11, 14, 13, 16, 15, 18, 17]
POPS = len(VELOCITY)
PAD = 8
FACES = [(1, 0), (-1, 0), (0, 1), (0, -1)]
CORNERS = [(1, 1), (-1, -1), (1, -1), (-1, 1)]
NEIGHBOURS = FACES + CORNERS
CROSSING = [
    [p for p in range(POPS) if VELOCITY[p][0] == 1],
    [p for p in range(POPS) if VELOCITY[p][0] == -1],
    [p for p in range(POPS) if VELOCITY[p][1] == 1],
    [p for p in range(POPS) if VELOCITY[p][1] == -1],
]


def total(terms):
    while len(terms) > 1:
        pairs = [a + b for a, b in zip(terms[::2], terms[1::2])]
        terms = pairs + ([terms[-1]] if len(terms) % 2 else [])
    return terms[0]


def collide(values, rate):
    edge = [values[p] for p in range(7, POPS)]
    density = 1.0 + (
        (1.0 / 3.0) * values[0] + (1.0 / 18.0) * total(values[1:7]) + (1.0 / 36.0) * total(edge)
    )
    inverse = 1.0 / density
    speeds = []
    for axis in range(3):
        face = None
        diagonal = None
        for p in range(1, POPS, 2):
            sign = VELOCITY[p][axis]
            if sign == 0:
                continue
            difference = values[p] - values[p + 1]
            if p < 7:
                face = difference if sign == 1 else -difference
            elif diagonal is None:
                diagonal = difference if sign == 1 else -difference
            else:
                diagonal = diagonal + difference if sign == 1 else diagonal - difference
        speeds.append(((1.0 / 18.0) * face + (1.0 / 36.0) * diagonal) * inverse)
    square = speeds[0] * speeds[0] + speeds[1] * speeds[1] + speeds[2] * speeds[2]
    keep = 1.0 - rate
    scaled = rate * density
    base = scaled * (1.0 - 1.5 * square) - rate
    results = [keep * values[0] + base]
    for p in range(1, POPS, 2):
        project = None
        for axis in range(3):
            sign = VELOCITY[p][axis]
            if sign == 0:
                continue
            if project is None:
                project = speeds[axis] if sign == 1 else -speeds[axis]
            else:
                project = project + speeds[axis] if sign == 1 else project - speeds[axis]
        even = base + scaled * (4.5 * project * project)
        odd = scaled * (3.0 * project)
        results.append(keep * values[p] + (even + odd))
        results.append(keep * values[p + 1] + (even - odd))
    return results


def steps_kernel(
    nx,
    ny,
    pop_ref,
    rate_ref,
    out_ref,
    first,
    second,
    x_send,
    x_recv,
    y_send,
    y_recv,
    c_send,
    c_recv,
    send_sem,
    recv_sem,
):
    nz = pop_ref.shape[3]
    gx = lax.axis_index("gx")
    yz = lax.axis_index("yz")
    gx_count = lax.axis_size("gx")
    yz_count = lax.axis_size("yz")

    def device(offset):
        return (
            lax.rem(gx + offset[0] + gx_count, gx_count),
            lax.rem(yz + offset[1] + yz_count, yz_count),
        )

    barrier = pltpu.get_barrier_semaphore()
    for offset in NEIGHBOURS:
        pl.semaphore_signal(barrier, inc=1, device_id=device(offset), device_id_type=MESH)
    lane = lax.broadcasted_iota(jnp.int32, (BS, nz), 1)

    def put(target, x, start, collided):
        for p in range(POPS):
            rounded = collided[p].astype(jnp.bfloat16).astype(jnp.float32)
            target[p, x + 1, PAD + start : PAD + start + BS, :] = rounded

    def gather(source, x, start):
        values = []
        for p in range(POPS):
            dx, dy, dz = VELOCITY[p]
            low = PAD + start - dy
            value = source[p, x + 1 - dx, low : low + BS, :]
            if dz != 0:
                mirror = source[OPPOSITE[p], x + 1, PAD + start : PAD + start + BS, :]
                if dz == 1:
                    value = jnp.where(lane == 0, mirror, pltpu.roll(value, 1, axis=1))
                else:
                    value = jnp.where(lane == nz - 1, mirror, pltpu.roll(value, nz - 1, axis=1))
            values.append(value)
        return values

    def exchange(step, field):
        for side in range(2):
            plane = nx if side == 0 else 1
            row = PAD + ny - 1 if side == 0 else PAD
            for k, p in enumerate(CROSSING[side]):
                x_send[step, side, k] = field[p, plane, PAD : PAD + ny, :]

        def pack(x, carry):
            for side in range(2):
                row = PAD + ny - 1 if side == 0 else PAD
                for k, p in enumerate(CROSSING[2 + side]):
                    y_send[step, side, k, pl.ds(x, 1), :] = field[p, x + 1, row : row + 1, :]
            return carry

        lax.fori_loop(0, nx, pack, 0)
        for c, (dx, dy) in enumerate(CORNERS):
            low = ny if dy == 1 else PAD
            c_send[step, c] = field[7 + c, nx if dx == 1 else 1, low : low + PAD, :]
        if step == 0:
            pl.semaphore_wait(barrier, len(NEIGHBOURS))
        copies = []
        for n, offset in enumerate(NEIGHBOURS):
            if n < 2:
                pair = (x_send.at[step, n], x_recv.at[step, n])
            elif n < 4:
                pair = (y_send.at[step, n - 2], y_recv.at[step, n - 2])
            else:
                pair = (c_send.at[step, n - 4], c_recv.at[step, n - 4])
            copy = pltpu.make_async_remote_copy(
                src_ref=pair[0],
                dst_ref=pair[1],
                send_sem=send_sem.at[step, n],
                recv_sem=recv_sem.at[step, n],
                device_id=device(offset),
                device_id_type=MESH,
            )
            copy.start()
            copies.append(copy)
        for copy in copies:
            copy.wait()
        for side in range(2):
            for k, p in enumerate(CROSSING[side]):
                field[p, 0 if side == 0 else nx + 1, PAD : PAD + ny, :] = x_recv[step, side, k]

        def unpack(x, carry):
            for side in range(2):
                row = PAD - 1 if side == 0 else PAD + ny
                for k, p in enumerate(CROSSING[2 + side]):
                    field[p, x + 1, row : row + 1, :] = y_recv[step, side, k, pl.ds(x, 1), :]
            return carry

        lax.fori_loop(0, nx, unpack, 0)
        for c, (dx, dy) in enumerate(CORNERS):
            low = 0 if dy == 1 else PAD + ny
            field[7 + c, 0 if dx == 1 else nx + 1, low : low + PAD, :] = c_recv[step, c]

    starts = range(0, ny, BS)

    def begin(x, carry):
        for start in starts:
            values = [pop_ref[p, x, start : start + BS, :].astype(jnp.float32) for p in range(POPS)]
            put(first, x, start, collide(values, rate_ref[start : start + BS, :]))
        return carry

    def middle(x, carry):
        for start in starts:
            values = gather(first, x, start)
            put(second, x, start, collide(values, rate_ref[start : start + BS, :]))
        return carry

    def finish(x, carry):
        for start in starts:
            values = gather(second, x, start)
            for p in range(POPS):
                out_ref[p, x, start : start + BS, :] = values[p].astype(jnp.bfloat16)
        return carry

    lax.fori_loop(0, nx, begin, 0)
    exchange(0, first)
    lax.fori_loop(0, nx, middle, 0)
    exchange(1, second)
    lax.fori_loop(0, nx, finish, 0)


def run_steps(populations, rates):
    _, nx, ny, nz = populations.shape
    field = pltpu.VMEM((POPS, nx + 2, ny + 2 * PAD, nz), jnp.float32)
    x_face = pltpu.VMEM((2, 2, 5, ny, nz), jnp.float32)
    y_face = pltpu.VMEM((2, 2, 5, nx, nz), jnp.float32)
    corner = pltpu.VMEM((2, 4, PAD, nz), jnp.float32)
    return pl.pallas_call(
        functools.partial(steps_kernel, nx, ny),
        out_shape=jax.ShapeDtypeStruct(populations.shape, jnp.bfloat16),
        in_specs=[pl.BlockSpec(memory_space=pltpu.VMEM)] * 2,
        out_specs=pl.BlockSpec(memory_space=pltpu.VMEM),
        scratch_shapes=[
            field,
            field,
            x_face,
            x_face,
            y_face,
            y_face,
            corner,
            corner,
            pltpu.SemaphoreType.DMA((2, len(NEIGHBOURS))),
            pltpu.SemaphoreType.DMA((2, len(NEIGHBOURS))),
        ],
        compiler_params=pltpu.CompilerParams(
            collective_id=0, has_side_effects=True, vmem_limit_bytes=48 * 2**20
        ),
        name="steps",
    )(populations, rates)


ROWS = 32
CHUNK = 4


def layout_kernel(nx, ny, nz, state_ref, select_ref, pool_ref, fine, packed):
    eighths = ny // 8
    across = nz // BS
    fine[...] = jnp.zeros_like(fine)

    def part(c, carry):
        for inner in range(CHUNK):
            x = c * CHUNK + inner
            for p in range(POPS):
                fine[p * ny : (p + 1) * ny, :] = state_ref[p, x].astype(jnp.float32)
            for e in range(eighths):
                row = (inner * eighths + e) * ROWS
                for j in range(8):
                    rows = fine[pl.ds(e * 8 + j, ROWS, stride=ny), :]
                    packed[row : row + ROWS, j * nz : (j + 1) * nz] = rows.astype(jnp.bfloat16)
        result = jnp.dot(packed[...], select_ref[...], preferred_element_type=jnp.float32)
        result = result.astype(jnp.bfloat16)
        for inner in range(CHUNK):
            for e in range(eighths):
                row = (inner * eighths + e) * ROWS
                lanes = pl.ds(pl.multiple_of((c * CHUNK * 2 + inner * 2 + e % 2) * 128, 128), 128)
                for k in range(across):
                    pool_ref[e // 2 * across + k, :, lanes] = result[
                        row : row + POPS, k * 128 : (k + 1) * 128
                    ]
        return carry

    lax.fori_loop(0, nx // CHUNK, part, 0)


def lay_out(state):
    _, nx, ny, nz = state.shape
    across = nz // BS
    select = np.zeros((8 * nz, across * 128), np.float32)
    for j in range(8):
        for z in range(nz):
            select[j * nz + z, z // BS * 128 + j * BS + z % BS] = 1.0
    blocks = ny // BS * across
    return pl.pallas_call(
        functools.partial(layout_kernel, nx, ny, nz),
        out_shape=jax.ShapeDtypeStruct((blocks, POPS, BS**3), jnp.bfloat16),
        in_specs=[pl.BlockSpec(memory_space=pltpu.VMEM)] * 2,
        out_specs=pl.BlockSpec(memory_space=pltpu.VMEM),
        scratch_shapes=[
            pltpu.VMEM((ROWS * ny, nz), jnp.float32),
            pltpu.VMEM((CHUNK * (ny // 8) * ROWS, 8 * nz), jnp.bfloat16),
        ],
        compiler_params=pltpu.CompilerParams(vmem_limit_bytes=32 * 2**20),
        cost_estimate=pl.CostEstimate(
            flops=2 * state.size * across * 128, bytes_accessed=8 * state.size, transcendentals=0
        ),
        name="layout",
    )(state, jnp.asarray(select, jnp.bfloat16))


LANES = BS**3 // 128
QUADS = HALF // 2


def merge_kernel(nx, ny, leaving_ref, state_ref, shrink_ref, select_ref, out_ref, fine, packed, held):
    nz = state_ref.shape[3]
    rows = ny // BS
    across = nz // BS
    groups = nx // 4
    fine[...] = jnp.zeros_like(fine)
    for p in range(POPS):
        planes = [
            jnp.concatenate([state_ref[p, g * 4 + i] for i in range(4)], axis=1)
            for g in range(groups)
        ]
        fine[p * groups * ny : (p + 1) * groups * ny, :] = jnp.dot(
            jnp.concatenate(planes, axis=0), shrink_ref[...], preferred_element_type=jnp.float32
        )
    for g in range(groups):
        for r in range(rows):
            row = (g * rows + r) * ROWS
            for j in range(HALF):
                start = g * ny + r * BS + 2 * j
                value = (
                    fine[pl.ds(start, ROWS, stride=groups * ny), :]
                    + fine[pl.ds(start + 1, ROWS, stride=groups * ny), :]
                )
                packed[row : row + ROWS, j * 128 : (j + 1) * 128] = value.astype(jnp.bfloat16)
    result = jnp.dot(packed[...], select_ref[...], preferred_element_type=jnp.float32)
    result = result.astype(jnp.bfloat16)
    for g in range(groups):
        for r in range(rows):
            row = (g * rows + r) * ROWS
            for k in range(across):
                held[r * across + k, :, g * 128 : (g + 1) * 128] = result[
                    row : row + POPS, k * 128 : (k + 1) * 128
                ]

    def give(target, carry):
        out_ref[target] = held[leaving_ref[target]]
        return carry

    lax.fori_loop(0, out_ref.shape[0], give, 0)


def merge(leaving, state):
    _, nx, ny, nz = state.shape
    across = nz // BS
    shrink = np.zeros((4, nz, 2, across, HALF), np.float32)
    for i in range(4):
        for z in range(nz):
            shrink[i, z, i // 2, z // BS, z % BS // 2] = 0.125
    shrink = shrink.reshape(4 * nz, 2 * across * HALF)
    select = np.zeros((HALF, 2, across, HALF, across, 2, HALF, HALF), np.float32)
    for j in range(HALF):
        for half in range(2):
            for k in range(across):
                for z in range(HALF):
                    select[j, half, k, z, k, half, j, z] = 1.0
    select = select.reshape(HALF * 2 * across * HALF, across * 128)
    blocks = ny // BS * across
    groups = nx // 4
    return pl.pallas_call(
        functools.partial(merge_kernel, nx, ny),
        out_shape=jax.ShapeDtypeStruct((leaving.shape[0], POPS, HALF**3), jnp.bfloat16),
        in_specs=[pl.BlockSpec(memory_space=pltpu.SMEM)]
        + [pl.BlockSpec(memory_space=pltpu.VMEM)] * 3,
        out_specs=pl.BlockSpec(memory_space=pltpu.VMEM),
        scratch_shapes=[
            pltpu.VMEM((ROWS * groups * ny, 128), jnp.float32),
            pltpu.VMEM((groups * (ny // BS) * ROWS, HALF * 128), jnp.bfloat16),
            pltpu.VMEM((blocks, POPS, HALF**3), jnp.bfloat16),
        ],
        compiler_params=pltpu.CompilerParams(vmem_limit_bytes=32 * 2**20),
        name="merge",
    )(leaving, state, jnp.asarray(shrink, jnp.bfloat16), jnp.asarray(select, jnp.bfloat16))


def fill_kernel(
    source_ref, origin_ref, kind_ref, pool_ref, incoming_ref, spread_ref, out_ref, held, packed, wide
):
    blocks = pool_ref.shape[0]
    arrivals = origin_ref.shape[0]
    packed[...] = jnp.zeros_like(packed)

    def load(a, carry):
        kind = kind_ref[a]
        value = incoming_ref[origin_ref[a]]
        zero = jnp.zeros_like(value)
        for half in range(2):
            part = jnp.where(kind == half + 1, value, zero)
            for q in range(QUADS):
                packed[a * QUADS + q, 0:POPS, half * 128 : (half + 1) * 128] = part[
                    :, q * 128 : (q + 1) * 128
                ]
        return carry

    lax.fori_loop(0, arrivals, load, 0)

    def expand(a, carry):
        rows = packed[pl.ds(a * 4 * QUADS, 4 * QUADS)].reshape(4 * QUADS * ROWS, 256)
        product = jnp.dot(rows, spread_ref[...], preferred_element_type=jnp.float32)
        wide[pl.ds(a * 4 * QUADS, 4 * QUADS)] = product.reshape(4 * QUADS, ROWS, 4 * 128)
        return carry

    lax.fori_loop(0, arrivals // 4, expand, 0)

    def place(slot, carry):
        source = source_ref[slot]
        rows = pl.ds(slot, POPS, stride=CAP)

        @pl.when(source < blocks)
        def _():
            value = pool_ref[jnp.minimum(source, blocks - 1)].astype(jnp.float32)
            for k in range(LANES):
                held[k, rows, :] = value[:, k * 128 : (k + 1) * 128]

        @pl.when((source >= blocks) & (source < blocks + arrivals))
        def _():
            index = jnp.clip(source - blocks, 0, arrivals - 1)
            linear = kind_ref[index] == 2
            near = jnp.where(linear, 0.75, 1.0)
            far = jnp.where(linear, 0.25, 0.0)
            for part in range(2):
                slabs = []
                for h in range(HALF):
                    lane = h % 2 * 256 + part * 128
                    slabs.append(wide[index * QUADS + h // 2, 0:POPS, lane : lane + 128])
                for x in range(BS):
                    h = x // 2
                    other = max(h - 1, 0) if x % 2 == 0 else min(h + 1, HALF - 1)
                    held[x * 2 + part, rows, :] = near * slabs[h] + far * slabs[other]

        @pl.when(source >= blocks + arrivals)
        def _():
            for k in range(LANES):
                held[k, rows, :] = jnp.zeros((POPS, 128), jnp.float32)

        return carry

    lax.fori_loop(0, CAP, place, 0)

    def emit(p, carry):
        rows = pl.ds(pl.multiple_of(p * CAP, 8), CAP)
        for k in range(LANES):
            out_ref[p, :, k * 128 : (k + 1) * 128] = held[k, rows, :].astype(jnp.bfloat16)
        return carry

    lax.fori_loop(0, POPS, emit, 0)


def fill(source, origin, kinds, pool, incoming):
    parent = np.arange(BS) // 2
    step = np.where(np.arange(BS) % 2 == 0, -1, 1)
    neighbour = np.clip(parent + step, 0, HALF - 1)
    inject = (parent[:, None] == np.arange(HALF)[None, :]).astype(np.float32)
    linear = 0.75 * inject + 0.25 * (neighbour[:, None] == np.arange(HALF)[None, :])
    spread = np.concatenate(
        [np.kron(np.eye(2), np.kron(matrix, matrix).T) for matrix in (inject, linear)], axis=0
    )
    count = origin.shape[0]
    slotted = pl.pallas_call(
        fill_kernel,
        out_shape=jax.ShapeDtypeStruct((POPS, CAP, BS**3), jnp.bfloat16),
        in_specs=[pl.BlockSpec(memory_space=pltpu.SMEM)] * 3
        + [pl.BlockSpec(memory_space=pltpu.VMEM)] * 3,
        out_specs=pl.BlockSpec(memory_space=pltpu.VMEM),
        scratch_shapes=[
            pltpu.VMEM((LANES, POPS * CAP, 128), jnp.float32),
            pltpu.VMEM((count * QUADS, ROWS, 256), jnp.bfloat16),
            pltpu.VMEM((count * QUADS, ROWS, 512), jnp.float32),
        ],
        compiler_params=pltpu.CompilerParams(vmem_limit_bytes=48 * 2**20),
        name="fill",
    )(source, origin, kinds, pool, incoming, jnp.asarray(spread, jnp.bfloat16))
    return jnp.transpose(slotted, (1, 0, 2))


def body(populations, levels, refine_flags, new_owner):
    slab_count = lax.axis_size("gx")
    column_count = lax.axis_size("yz")
    slab = lax.axis_index("gx")
    column = lax.axis_index("yz")
    me = slab * column_count + column
    devices = slab_count * column_count
    _, nx, ny, nz = populations.shape
    across = nz // BS
    rows = ny // BS
    local = rows * across
    base = me * local
    block_total = new_owner.shape[0]

    local_levels = lax.dynamic_slice(levels, (base,), (local,)).reshape(rows, across)
    block_rates = 1.0 / (0.5 + jnp.power(0.5, local_levels.astype(jnp.float32)))
    rates = jnp.repeat(jnp.repeat(block_rates, BS, 0), BS, 1)

    ids = jnp.arange(block_total, dtype=jnp.int32)
    owned = new_owner == me
    before = owned[None, :] & (ids[None, :] < ids[:, None])
    rank = jnp.sum(before.astype(jnp.int32), axis=1)
    slots = jnp.arange(CAP, dtype=jnp.int32)
    hit = owned[None, :] & (rank[None, :] == slots[:, None])
    slot_id = jnp.sum(jnp.where(hit, ids[None, :], 0), axis=1)
    slot_kind = jnp.sum(jnp.where(hit, refine_flags[None, :], 0), axis=1)
    slot_used = jnp.any(hit, axis=1)
    flagged = slot_kind != 0
    slot_rank = jnp.sum(
        (flagged[None, :] & (slots[None, :] < slots[:, None])).astype(jnp.int32), axis=1
    )
    order = jnp.arange(2 * MIG, dtype=jnp.int32)
    match = flagged[None, :] & (slot_rank[None, :] == order[:, None])
    arrival_id = jnp.sum(jnp.where(match, slot_id[None, :], 0), axis=1)
    arrival_kind = jnp.sum(jnp.where(match, slot_kind[None, :], 0), axis=1)
    source = jnp.where(
        slot_used,
        jnp.where(flagged, local + slot_rank, slot_id % local),
        local + 2 * MIG,
    )

    local_flags = lax.dynamic_slice(refine_flags, (base,), (local,))
    local_owner = lax.dynamic_slice(new_owner, (base,), (local,))
    leaving = (local_flags != 0)[None, :] & (
        local_owner[None, :] == jnp.arange(devices, dtype=jnp.int32)[:, None]
    )
    leaving_block = jnp.sum(
        jnp.where(leaving, jnp.arange(local, dtype=jnp.int32)[None, :], 0), axis=1
    )

    state = run_steps(populations, rates)
    outgoing = merge(leaving_block, state)
    incoming = lax.all_to_all(outgoing, ("gx", "yz"), split_axis=0, concat_axis=0, tiled=True)
    pool = lay_out(state)
    return fill(source, arrival_id // local, arrival_kind, pool, incoming)


def solution(mesh):
    placed = (P(None, "gx", "yz", None), P(), P(), P())
    return jax.shard_map(
        body, mesh=mesh, in_specs=placed, out_specs=P(("gx", "yz"), None, None), check_vma=False
    )
```

```python
import functools

import jax
import jax.numpy as jnp
import numpy as np
from jax import lax
from jax.experimental import pallas as pl
from jax.experimental.pallas import tpu as pltpu
from jax.sharding import PartitionSpec as P

BS = 16
HALF = 8
MIG = 8
CAP = 24
MESH = pl.DeviceIdType.MESH

VELOCITY = [
    (0, 0, 0),
    (1, 0, 0),
    (-1, 0, 0),
    (0, 1, 0),
    (0, -1, 0),
    (0, 0, 1),
    (0, 0, -1),
    (1, 1, 0),
    (-1, -1, 0),
    (1, -1, 0),
    (-1, 1, 0),
    (1, 0, 1),
    (-1, 0, -1),
    (1, 0, -1),
    (-1, 0, 1),
    (0, 1, 1),
    (0, -1, -1),
    (0, 1, -1),
    (0, -1, 1),
]
WEIGHT = [1.0 / 3.0] + [1.0 / 18.0] * 6 + [1.0 / 36.0] * 12
OPPOSITE = [0, 2, 1, 4, 3, 6, 5, 8, 7, 10, 9, 12, 11, 14, 13, 16, 15, 18, 17]
POPS = len(VELOCITY)
PAD = 8
FACES = [(1, 0), (-1, 0), (0, 1), (0, -1)]
CORNERS = [(1, 1), (-1, -1), (1, -1), (-1, 1)]
NEIGHBOURS = FACES + CORNERS
CROSSING = [
    [p for p in range(POPS) if VELOCITY[p][0] == 1],
    [p for p in range(POPS) if VELOCITY[p][0] == -1],
    [p for p in range(POPS) if VELOCITY[p][1] == 1],
    [p for p in range(POPS) if VELOCITY[p][1] == -1],
]


def total(terms):
    while len(terms) > 1:
        pairs = [a + b for a, b in zip(terms[::2], terms[1::2])]
        terms = pairs + ([terms[-1]] if len(terms) % 2 else [])
    return terms[0]


def collide(values, rate):
    edge = [values[p] for p in range(7, POPS)]
    density = 1.0 + (
        (1.0 / 3.0) * values[0] + (1.0 / 18.0) * total(values[1:7]) + (1.0 / 36.0) * total(edge)
    )
    inverse = 1.0 / density
    speeds = []
    for axis in range(3):
        face = None
        diagonal = None
        for p in range(1, POPS, 2):
            sign = VELOCITY[p][axis]
            if sign == 0:
                continue
            difference = values[p] - values[p + 1]
            if p < 7:
                face = difference if sign == 1 else -difference
            elif diagonal is None:
                diagonal = difference if sign == 1 else -difference
            else:
                diagonal = diagonal + difference if sign == 1 else diagonal - difference
        speeds.append(((1.0 / 18.0) * face + (1.0 / 36.0) * diagonal) * inverse)
    square = speeds[0] * speeds[0] + speeds[1] * speeds[1] + speeds[2] * speeds[2]
    keep = 1.0 - rate
    scaled = rate * density
    base = scaled * (1.0 - 1.5 * square) - rate
    results = [keep * values[0] + base]
    for p in range(1, POPS, 2):
        project = None
        for axis in range(3):
            sign = VELOCITY[p][axis]
            if sign == 0:
                continue
            if project is None:
                project = speeds[axis] if sign == 1 else -speeds[axis]
            else:
                project = project + speeds[axis] if sign == 1 else project - speeds[axis]
        even = base + scaled * (4.5 * project * project)
        odd = scaled * (3.0 * project)
        results.append(keep * values[p] + (even + odd))
        results.append(keep * values[p + 1] + (even - odd))
    return results


def steps_kernel(
    nx,
    ny,
    pop_ref,
    rate_ref,
    out_ref,
    first,
    second,
    x_send,
    x_recv,
    y_send,
    y_recv,
    c_send,
    c_recv,
    send_sem,
    recv_sem,
):
    nz = pop_ref.shape[3]
    gx = lax.axis_index("gx")
    yz = lax.axis_index("yz")
    gx_count = lax.axis_size("gx")
    yz_count = lax.axis_size("yz")

    def device(offset):
        return (
            lax.rem(gx + offset[0] + gx_count, gx_count),
            lax.rem(yz + offset[1] + yz_count, yz_count),
        )

    barrier = pltpu.get_barrier_semaphore()
    for offset in NEIGHBOURS:
        pl.semaphore_signal(barrier, inc=1, device_id=device(offset), device_id_type=MESH)
    def put(target, x, start, count, collided):
        for p in range(POPS):
            rounded = collided[p].astype(jnp.bfloat16).astype(jnp.float32)
            target[p, x + 1, PAD + start : PAD + start + count, :] = rounded

    def gather(source, x, start, count):
        lane = lax.broadcasted_iota(jnp.int32, (count, nz), 1)
        values = []
        for p in range(POPS):
            dx, dy, dz = VELOCITY[p]
            low = PAD + start - dy
            value = source[p, x + 1 - dx, low : low + count, :]
            if dz != 0:
                mirror = source[OPPOSITE[p], x + 1, PAD + start : PAD + start + count, :]
                if dz == 1:
                    value = jnp.where(lane == 0, mirror, pltpu.roll(value, 1, axis=1))
                else:
                    value = jnp.where(lane == nz - 1, mirror, pltpu.roll(value, nz - 1, axis=1))
            values.append(value)
        return values

    def send(step, first_index, pairs):
        copies = []
        for n, pair in enumerate(pairs, first_index):
            copy = pltpu.make_async_remote_copy(
                src_ref=pair[0],
                dst_ref=pair[1],
                send_sem=send_sem.at[step, n],
                recv_sem=recv_sem.at[step, n],
                device_id=device(NEIGHBOURS[n]),
                device_id_type=MESH,
            )
            copy.start()
            copies.append(copy)
        return copies

    def send_x(step, field):
        for side in range(2):
            plane = nx if side == 0 else 1
            for k, p in enumerate(CROSSING[side]):
                x_send[step, side, k] = field[p, plane, PAD : PAD + ny, :]
        for c, (dx, dy) in enumerate(CORNERS):
            low = ny if dy == 1 else PAD
            c_send[step, c] = field[7 + c, nx if dx == 1 else 1, low : low + PAD, :]
        if step == 0:
            pl.semaphore_wait(barrier, len(NEIGHBOURS))
        copies = send(step, 0, [(x_send.at[step, n], x_recv.at[step, n]) for n in range(2)])
        return copies + send(step, 4, [(c_send.at[step, n], c_recv.at[step, n]) for n in range(4)])

    def send_y(step, field):
        def pack(x, carry):
            for side in range(2):
                row = PAD + ny - 1 if side == 0 else PAD
                for k, p in enumerate(CROSSING[2 + side]):
                    y_send[step, side, k, pl.ds(x, 1), :] = field[p, x + 1, row : row + 1, :]
            return carry

        lax.fori_loop(0, nx, pack, 0)
        return send(step, 2, [(y_send.at[step, n], y_recv.at[step, n]) for n in range(2)])

    def take_x(step, field, copies):
        for copy in copies:
            copy.wait()
        for side in range(2):
            for k, p in enumerate(CROSSING[side]):
                field[p, 0 if side == 0 else nx + 1, PAD : PAD + ny, :] = x_recv[step, side, k]
        for c, (dx, dy) in enumerate(CORNERS):
            low = 0 if dy == 1 else PAD + ny
            field[7 + c, 0 if dx == 1 else nx + 1, low : low + PAD, :] = c_recv[step, c]

    def take_y(step, field, copies):
        for copy in copies:
            copy.wait()

        def unpack(x, carry):
            for side in range(2):
                row = PAD - 1 if side == 0 else PAD + ny
                for k, p in enumerate(CROSSING[2 + side]):
                    field[p, x + 1, row : row + 1, :] = y_recv[step, side, k, pl.ds(x, 1), :]
            return carry

        lax.fori_loop(0, nx, unpack, 0)

    def begin(x):
        for start in range(0, ny, BS):
            values = [pop_ref[p, x, start : start + BS, :].astype(jnp.float32) for p in range(POPS)]
            put(first, x, start, BS, collide(values, rate_ref[start : start + BS, :]))

    def middle(x, starts):
        for start in starts:
            values = gather(first, x, start, 8)
            put(second, x, start, 8, collide(values, rate_ref[start : start + 8, :]))

    def finish(x):
        for start in range(0, ny, BS):
            values = gather(second, x, start, BS)
            for p in range(POPS):
                out_ref[p, x, start : start + BS, :] = values[p].astype(jnp.bfloat16)

    def sweep(low, high, work):
        def one(x, carry):
            work(x)
            return carry

        lax.fori_loop(low, high, one, 0)

    inner = range(8, ny - 8, 8)
    outer = (0, ny - 8)
    sweep(0, 2, lambda i: begin(i * (nx - 1)))
    x_copies = send_x(0, first)
    sweep(1, nx - 1, begin)
    y_copies = send_y(0, first)
    take_x(0, first, x_copies)
    sweep(0, nx, lambda x: middle(x, inner))
    take_y(0, first, y_copies)
    sweep(0, 2, lambda i: middle(i * (nx - 1), outer))
    x_copies = send_x(1, second)
    sweep(1, nx - 1, lambda x: middle(x, outer))
    y_copies = send_y(1, second)
    take_x(1, second, x_copies)
    take_y(1, second, y_copies)
    sweep(0, nx, finish)


def run_steps(populations, rates):
    _, nx, ny, nz = populations.shape
    field = pltpu.VMEM((POPS, nx + 2, ny + 2 * PAD, nz), jnp.float32)
    x_face = pltpu.VMEM((2, 2, 5, ny, nz), jnp.float32)
    y_face = pltpu.VMEM((2, 2, 5, nx, nz), jnp.float32)
    corner = pltpu.VMEM((2, 4, PAD, nz), jnp.float32)
    return pl.pallas_call(
        functools.partial(steps_kernel, nx, ny),
        out_shape=jax.ShapeDtypeStruct(populations.shape, jnp.bfloat16),
        in_specs=[pl.BlockSpec(memory_space=pltpu.VMEM)] * 2,
        out_specs=pl.BlockSpec(memory_space=pltpu.VMEM),
        scratch_shapes=[
            field,
            field,
            x_face,
            x_face,
            y_face,
            y_face,
            corner,
            corner,
            pltpu.SemaphoreType.DMA((2, len(NEIGHBOURS))),
            pltpu.SemaphoreType.DMA((2, len(NEIGHBOURS))),
        ],
        compiler_params=pltpu.CompilerParams(
            collective_id=0, has_side_effects=True, vmem_limit_bytes=48 * 2**20
        ),
        name="steps",
    )(populations, rates)


ROWS = 32
CHUNK = 4


def layout_kernel(nx, ny, nz, state_ref, select_ref, pool_ref, fine, packed):
    eighths = ny // 8
    across = nz // BS
    fine[...] = jnp.zeros_like(fine)

    def part(c, carry):
        for inner in range(CHUNK):
            x = c * CHUNK + inner
            for p in range(POPS):
                fine[p * ny : (p + 1) * ny, :] = state_ref[p, x].astype(jnp.float32)
            for e in range(eighths):
                row = (inner * eighths + e) * ROWS
                for j in range(8):
                    rows = fine[pl.ds(e * 8 + j, ROWS, stride=ny), :]
                    packed[row : row + ROWS, j * nz : (j + 1) * nz] = rows.astype(jnp.bfloat16)
        result = jnp.dot(packed[...], select_ref[...], preferred_element_type=jnp.float32)
        result = result.astype(jnp.bfloat16)
        for inner in range(CHUNK):
            for e in range(eighths):
                row = (inner * eighths + e) * ROWS
                lanes = pl.ds(pl.multiple_of((c * CHUNK * 2 + inner * 2 + e % 2) * 128, 128), 128)
                for k in range(across):
                    pool_ref[e // 2 * across + k, :, lanes] = result[
                        row : row + POPS, k * 128 : (k + 1) * 128
                    ]
        return carry

    lax.fori_loop(0, nx // CHUNK, part, 0)


def lay_out(state):
    _, nx, ny, nz = state.shape
    across = nz // BS
    select = np.zeros((8 * nz, across * 128), np.float32)
    for j in range(8):
        for z in range(nz):
            select[j * nz + z, z // BS * 128 + j * BS + z % BS] = 1.0
    blocks = ny // BS * across
    return pl.pallas_call(
        functools.partial(layout_kernel, nx, ny, nz),
        out_shape=jax.ShapeDtypeStruct((blocks, POPS, BS**3), jnp.bfloat16),
        in_specs=[pl.BlockSpec(memory_space=pltpu.VMEM)] * 2,
        out_specs=pl.BlockSpec(memory_space=pltpu.VMEM),
        scratch_shapes=[
            pltpu.VMEM((ROWS * ny, nz), jnp.float32),
            pltpu.VMEM((CHUNK * (ny // 8) * ROWS, 8 * nz), jnp.bfloat16),
        ],
        compiler_params=pltpu.CompilerParams(vmem_limit_bytes=32 * 2**20),
        cost_estimate=pl.CostEstimate(
            flops=2 * state.size * across * 128, bytes_accessed=8 * state.size, transcendentals=0
        ),
        name="layout",
    )(state, jnp.asarray(select, jnp.bfloat16))


LANES = BS**3 // 128
QUADS = HALF // 2


def merge_kernel(nx, ny, leaving_ref, state_ref, shrink_ref, select_ref, out_ref, fine, packed, held):
    nz = state_ref.shape[3]
    rows = ny // BS
    across = nz // BS
    groups = nx // 4
    fine[...] = jnp.zeros_like(fine)
    for p in range(POPS):
        planes = [
            jnp.concatenate([state_ref[p, g * 4 + i] for i in range(4)], axis=1)
            for g in range(groups)
        ]
        fine[p * groups * ny : (p + 1) * groups * ny, :] = jnp.dot(
            jnp.concatenate(planes, axis=0), shrink_ref[...], preferred_element_type=jnp.float32
        )
    for g in range(groups):
        for r in range(rows):
            row = (g * rows + r) * ROWS
            for j in range(HALF):
                start = g * ny + r * BS + 2 * j
                value = (
                    fine[pl.ds(start, ROWS, stride=groups * ny), :]
                    + fine[pl.ds(start + 1, ROWS, stride=groups * ny), :]
                )
                packed[row : row + ROWS, j * 128 : (j + 1) * 128] = value.astype(jnp.bfloat16)
    result = jnp.dot(packed[...], select_ref[...], preferred_element_type=jnp.float32)
    result = result.astype(jnp.bfloat16)
    for g in range(groups):
        for r in range(rows):
            row = (g * rows + r) * ROWS
            for k in range(across):
                held[r * across + k, :, g * 128 : (g + 1) * 128] = result[
                    row : row + POPS, k * 128 : (k + 1) * 128
                ]

    def give(target, carry):
        out_ref[target] = held[leaving_ref[target]]
        return carry

    lax.fori_loop(0, out_ref.shape[0], give, 0)


def merge(leaving, state):
    _, nx, ny, nz = state.shape
    across = nz // BS
    shrink = np.zeros((4, nz, 2, across, HALF), np.float32)
    for i in range(4):
        for z in range(nz):
            shrink[i, z, i // 2, z // BS, z % BS // 2] = 0.125
    shrink = shrink.reshape(4 * nz, 2 * across * HALF)
    select = np.zeros((HALF, 2, across, HALF, across, 2, HALF, HALF), np.float32)
    for j in range(HALF):
        for half in range(2):
            for k in range(across):
                for z in range(HALF):
                    select[j, half, k, z, k, half, j, z] = 1.0
    select = select.reshape(HALF * 2 * across * HALF, across * 128)
    blocks = ny // BS * across
    groups = nx // 4
    return pl.pallas_call(
        functools.partial(merge_kernel, nx, ny),
        out_shape=jax.ShapeDtypeStruct((leaving.shape[0], POPS, HALF**3), jnp.bfloat16),
        in_specs=[pl.BlockSpec(memory_space=pltpu.SMEM)]
        + [pl.BlockSpec(memory_space=pltpu.VMEM)] * 3,
        out_specs=pl.BlockSpec(memory_space=pltpu.VMEM),
        scratch_shapes=[
            pltpu.VMEM((ROWS * groups * ny, 128), jnp.float32),
            pltpu.VMEM((groups * (ny // BS) * ROWS, HALF * 128), jnp.bfloat16),
            pltpu.VMEM((blocks, POPS, HALF**3), jnp.bfloat16),
        ],
        compiler_params=pltpu.CompilerParams(vmem_limit_bytes=32 * 2**20),
        name="merge",
    )(leaving, state, jnp.asarray(shrink, jnp.bfloat16), jnp.asarray(select, jnp.bfloat16))


def fill_kernel(
    source_ref,
    origin_ref,
    kind_ref,
    pool_source,
    incoming_ref,
    spread_ref,
    out_ref,
    held,
    packed,
    wide,
    pool_ref,
    pool_sem,
):
    fetch = pltpu.make_async_copy(pool_source, pool_ref, pool_sem)
    fetch.start()
    blocks = pool_ref.shape[0]
    arrivals = origin_ref.shape[0]
    packed[...] = jnp.zeros_like(packed)

    def load(a, carry):
        kind = kind_ref[a]
        value = incoming_ref[origin_ref[a]]
        zero = jnp.zeros_like(value)
        for half in range(2):
            part = jnp.where(kind == half + 1, value, zero)
            for q in range(QUADS):
                packed[a * QUADS + q, 0:POPS, half * 128 : (half + 1) * 128] = part[
                    :, q * 128 : (q + 1) * 128
                ]
        return carry

    lax.fori_loop(0, arrivals, load, 0)

    def expand(a, carry):
        rows = packed[pl.ds(a * 4 * QUADS, 4 * QUADS)].reshape(4 * QUADS * ROWS, 256)
        product = jnp.dot(rows, spread_ref[...], preferred_element_type=jnp.float32)
        wide[pl.ds(a * 4 * QUADS, 4 * QUADS)] = product.reshape(4 * QUADS, ROWS, 4 * 128)
        return carry

    lax.fori_loop(0, arrivals // 4, expand, 0)
    fetch.wait()

    def place(slot, carry):
        source = source_ref[slot]
        rows = pl.ds(slot, POPS, stride=CAP)

        @pl.when(source < blocks)
        def _():
            value = pool_ref[jnp.minimum(source, blocks - 1)].astype(jnp.float32)
            for k in range(LANES):
                held[k, rows, :] = value[:, k * 128 : (k + 1) * 128]

        @pl.when((source >= blocks) & (source < blocks + arrivals))
        def _():
            index = jnp.clip(source - blocks, 0, arrivals - 1)
            linear = kind_ref[index] == 2
            near = jnp.where(linear, 0.75, 1.0)
            far = jnp.where(linear, 0.25, 0.0)
            for part in range(2):
                slabs = []
                for h in range(HALF):
                    lane = h % 2 * 256 + part * 128
                    slabs.append(wide[index * QUADS + h // 2, 0:POPS, lane : lane + 128])
                for x in range(BS):
                    h = x // 2
                    other = max(h - 1, 0) if x % 2 == 0 else min(h + 1, HALF - 1)
                    held[x * 2 + part, rows, :] = near * slabs[h] + far * slabs[other]

        @pl.when(source >= blocks + arrivals)
        def _():
            for k in range(LANES):
                held[k, rows, :] = jnp.zeros((POPS, 128), jnp.float32)

        return carry

    lax.fori_loop(0, CAP, place, 0)

    def emit(p, carry):
        rows = pl.ds(pl.multiple_of(p * CAP, 8), CAP)
        for k in range(LANES):
            out_ref[p, :, k * 128 : (k + 1) * 128] = held[k, rows, :].astype(jnp.bfloat16)
        return carry

    lax.fori_loop(0, POPS, emit, 0)


def fill(source, origin, kinds, pool, incoming):
    parent = np.arange(BS) // 2
    step = np.where(np.arange(BS) % 2 == 0, -1, 1)
    neighbour = np.clip(parent + step, 0, HALF - 1)
    inject = (parent[:, None] == np.arange(HALF)[None, :]).astype(np.float32)
    linear = 0.75 * inject + 0.25 * (neighbour[:, None] == np.arange(HALF)[None, :])
    spread = np.concatenate(
        [np.kron(np.eye(2), np.kron(matrix, matrix).T) for matrix in (inject, linear)], axis=0
    )
    count = origin.shape[0]
    slotted = pl.pallas_call(
        fill_kernel,
        out_shape=jax.ShapeDtypeStruct((POPS, CAP, BS**3), jnp.bfloat16),
        in_specs=[pl.BlockSpec(memory_space=pltpu.SMEM)] * 3
        + [pl.BlockSpec(memory_space=pl.ANY)]
        + [pl.BlockSpec(memory_space=pltpu.VMEM)] * 2,
        out_specs=pl.BlockSpec(memory_space=pltpu.VMEM),
        scratch_shapes=[
            pltpu.VMEM((LANES, POPS * CAP, 128), jnp.float32),
            pltpu.VMEM((count * QUADS, ROWS, 256), jnp.bfloat16),
            pltpu.VMEM((count * QUADS, ROWS, 512), jnp.float32),
            pltpu.VMEM(pool.shape, jnp.bfloat16),
            pltpu.SemaphoreType.DMA(()),
        ],
        compiler_params=pltpu.CompilerParams(vmem_limit_bytes=48 * 2**20),
        name="fill",
    )(source, origin, kinds, pool, incoming, jnp.asarray(spread, jnp.bfloat16))
    return jnp.transpose(slotted, (1, 0, 2))


def body(populations, levels, refine_flags, new_owner):
    slab_count = lax.axis_size("gx")
    column_count = lax.axis_size("yz")
    slab = lax.axis_index("gx")
    column = lax.axis_index("yz")
    me = slab * column_count + column
    devices = slab_count * column_count
    _, nx, ny, nz = populations.shape
    across = nz // BS
    rows = ny // BS
    local = rows * across
    base = me * local
    block_total = new_owner.shape[0]

    local_levels = lax.dynamic_slice(levels, (base,), (local,)).reshape(rows, across)
    block_rates = 1.0 / (0.5 + jnp.power(0.5, local_levels.astype(jnp.float32)))
    rates = jnp.repeat(jnp.repeat(block_rates, BS, 0), BS, 1)

    ids = jnp.arange(block_total, dtype=jnp.int32)
    owned = new_owner == me
    before = owned[None, :] & (ids[None, :] < ids[:, None])
    rank = jnp.sum(before.astype(jnp.int32), axis=1)
    slots = jnp.arange(CAP, dtype=jnp.int32)
    hit = owned[None, :] & (rank[None, :] == slots[:, None])
    slot_id = jnp.sum(jnp.where(hit, ids[None, :], 0), axis=1)
    slot_kind = jnp.sum(jnp.where(hit, refine_flags[None, :], 0), axis=1)
    slot_used = jnp.any(hit, axis=1)
    flagged = slot_kind != 0
    slot_rank = jnp.sum(
        (flagged[None, :] & (slots[None, :] < slots[:, None])).astype(jnp.int32), axis=1
    )
    order = jnp.arange(2 * MIG, dtype=jnp.int32)
    match = flagged[None, :] & (slot_rank[None, :] == order[:, None])
    arrival_id = jnp.sum(jnp.where(match, slot_id[None, :], 0), axis=1)
    arrival_kind = jnp.sum(jnp.where(match, slot_kind[None, :], 0), axis=1)
    source = jnp.where(
        slot_used,
        jnp.where(flagged, local + slot_rank, slot_id % local),
        local + 2 * MIG,
    )

    local_flags = lax.dynamic_slice(refine_flags, (base,), (local,))
    local_owner = lax.dynamic_slice(new_owner, (base,), (local,))
    leaving = (local_flags != 0)[None, :] & (
        local_owner[None, :] == jnp.arange(devices, dtype=jnp.int32)[:, None]
    )
    leaving_block = jnp.sum(
        jnp.where(leaving, jnp.arange(local, dtype=jnp.int32)[None, :], 0), axis=1
    )

    state = run_steps(populations, rates)
    outgoing = merge(leaving_block, state)
    incoming = lax.all_to_all(outgoing, ("gx", "yz"), split_axis=0, concat_axis=0, tiled=True)
    pool = lay_out(state)
    return fill(source, arrival_id // local, arrival_kind, pool, incoming)


def solution(mesh):
    placed = (P(None, "gx", "yz", None), P(), P(), P())
    return jax.shard_map(
        body, mesh=mesh, in_specs=placed, out_specs=P(("gx", "yz"), None, None), check_vma=False
    )
```

```python
import functools

import jax
import jax.numpy as jnp
import numpy as np
from jax import lax
from jax.experimental import pallas as pl
from jax.experimental.pallas import tpu as pltpu
from jax.sharding import PartitionSpec as P

BS = 16
HALF = 8
MIG = 8
CAP = 24
MESH = pl.DeviceIdType.MESH

VELOCITY = [
    (0, 0, 0),
    (1, 0, 0),
    (-1, 0, 0),
    (0, 1, 0),
    (0, -1, 0),
    (0, 0, 1),
    (0, 0, -1),
    (1, 1, 0),
    (-1, -1, 0),
    (1, -1, 0),
    (-1, 1, 0),
    (1, 0, 1),
    (-1, 0, -1),
    (1, 0, -1),
    (-1, 0, 1),
    (0, 1, 1),
    (0, -1, -1),
    (0, 1, -1),
    (0, -1, 1),
]
WEIGHT = [1.0 / 3.0] + [1.0 / 18.0] * 6 + [1.0 / 36.0] * 12
OPPOSITE = [0, 2, 1, 4, 3, 6, 5, 8, 7, 10, 9, 12, 11, 14, 13, 16, 15, 18, 17]
POPS = len(VELOCITY)
PAD = 8
FACES = [(1, 0), (-1, 0), (0, 1), (0, -1)]
CORNERS = [(1, 1), (-1, -1), (1, -1), (-1, 1)]
NEIGHBOURS = FACES + CORNERS
CROSSING = [
    [p for p in range(POPS) if VELOCITY[p][0] == 1],
    [p for p in range(POPS) if VELOCITY[p][0] == -1],
    [p for p in range(POPS) if VELOCITY[p][1] == 1],
    [p for p in range(POPS) if VELOCITY[p][1] == -1],
]


def total(terms):
    while len(terms) > 1:
        pairs = [a + b for a, b in zip(terms[::2], terms[1::2])]
        terms = pairs + ([terms[-1]] if len(terms) % 2 else [])
    return terms[0]


def collide(values, rate):
    edge = [values[p] for p in range(7, POPS)]
    density = 1.0 + (
        (1.0 / 3.0) * values[0] + (1.0 / 18.0) * total(values[1:7]) + (1.0 / 36.0) * total(edge)
    )
    inverse = 1.0 / density
    speeds = []
    for axis in range(3):
        face = None
        diagonal = None
        for p in range(1, POPS, 2):
            sign = VELOCITY[p][axis]
            if sign == 0:
                continue
            difference = values[p] - values[p + 1]
            if p < 7:
                face = difference if sign == 1 else -difference
            elif diagonal is None:
                diagonal = difference if sign == 1 else -difference
            else:
                diagonal = diagonal + difference if sign == 1 else diagonal - difference
        speeds.append(((1.0 / 18.0) * face + (1.0 / 36.0) * diagonal) * inverse)
    square = speeds[0] * speeds[0] + speeds[1] * speeds[1] + speeds[2] * speeds[2]
    keep = 1.0 - rate
    scaled = rate * density
    base = scaled * (1.0 - 1.5 * square) - rate
    results = [keep * values[0] + base]
    for p in range(1, POPS, 2):
        project = None
        for axis in range(3):
            sign = VELOCITY[p][axis]
            if sign == 0:
                continue
            if project is None:
                project = speeds[axis] if sign == 1 else -speeds[axis]
            else:
                project = project + speeds[axis] if sign == 1 else project - speeds[axis]
        even = base + scaled * (4.5 * project * project)
        odd = scaled * (3.0 * project)
        results.append(keep * values[p] + (even + odd))
        results.append(keep * values[p + 1] + (even - odd))
    return results


def steps_kernel(
    nx,
    ny,
    pop_ref,
    rate_ref,
    out_ref,
    first,
    second,
    x_send,
    x_recv,
    y_send,
    y_recv,
    c_send,
    c_recv,
    send_sem,
    recv_sem,
):
    nz = pop_ref.shape[3]
    gx = lax.axis_index("gx")
    yz = lax.axis_index("yz")
    gx_count = lax.axis_size("gx")
    yz_count = lax.axis_size("yz")

    def device(offset):
        return (
            lax.rem(gx + offset[0] + gx_count, gx_count),
            lax.rem(yz + offset[1] + yz_count, yz_count),
        )

    barrier = pltpu.get_barrier_semaphore()
    for offset in NEIGHBOURS:
        pl.semaphore_signal(barrier, inc=1, device_id=device(offset), device_id_type=MESH)
    def put(target, x, start, count, collided):
        for p in range(POPS):
            rounded = collided[p].astype(jnp.bfloat16).astype(jnp.float32)
            target[p, x + 1, PAD + start : PAD + start + count, :] = rounded

    def gather(source, x, start, count):
        lane = lax.broadcasted_iota(jnp.int32, (count, nz), 1)
        values = []
        for p in range(POPS):
            dx, dy, dz = VELOCITY[p]
            low = PAD + start - dy
            value = source[p, x + 1 - dx, low : low + count, :]
            if dz != 0:
                mirror = source[OPPOSITE[p], x + 1, PAD + start : PAD + start + count, :]
                if dz == 1:
                    value = jnp.where(lane == 0, mirror, pltpu.roll(value, 1, axis=1))
                else:
                    value = jnp.where(lane == nz - 1, mirror, pltpu.roll(value, nz - 1, axis=1))
            values.append(value)
        return values

    def send(step, first_index, pairs):
        copies = []
        for n, pair in enumerate(pairs, first_index):
            copy = pltpu.make_async_remote_copy(
                src_ref=pair[0],
                dst_ref=pair[1],
                send_sem=send_sem.at[step, n],
                recv_sem=recv_sem.at[step, n],
                device_id=device(NEIGHBOURS[n]),
                device_id_type=MESH,
            )
            copy.start()
            copies.append(copy)
        return copies

    def send_x(step, field):
        for side in range(2):
            plane = nx if side == 0 else 1
            for k, p in enumerate(CROSSING[side]):
                x_send[step, side, k] = field[p, plane, PAD : PAD + ny, :]
        for c, (dx, dy) in enumerate(CORNERS):
            low = ny if dy == 1 else PAD
            c_send[step, c] = field[7 + c, nx if dx == 1 else 1, low : low + PAD, :]
        if step == 0:
            pl.semaphore_wait(barrier, len(NEIGHBOURS))
        copies = send(step, 0, [(x_send.at[step, n], x_recv.at[step, n]) for n in range(2)])
        return copies + send(step, 4, [(c_send.at[step, n], c_recv.at[step, n]) for n in range(4)])

    def send_y(step, field):
        def pack(x, carry):
            for side in range(2):
                row = PAD + ny - 1 if side == 0 else PAD
                for k, p in enumerate(CROSSING[2 + side]):
                    y_send[step, side, k, pl.ds(x, 1), :] = field[p, x + 1, row : row + 1, :]
            return carry

        lax.fori_loop(0, nx, pack, 0)
        return send(step, 2, [(y_send.at[step, n], y_recv.at[step, n]) for n in range(2)])

    def take_x(step, field, copies):
        for copy in copies:
            copy.wait()
        for side in range(2):
            for k, p in enumerate(CROSSING[side]):
                field[p, 0 if side == 0 else nx + 1, PAD : PAD + ny, :] = x_recv[step, side, k]
        for c, (dx, dy) in enumerate(CORNERS):
            low = 0 if dy == 1 else PAD + ny
            field[7 + c, 0 if dx == 1 else nx + 1, low : low + PAD, :] = c_recv[step, c]

    def take_y(step, field, copies):
        for copy in copies:
            copy.wait()

        def unpack(x, carry):
            for side in range(2):
                row = PAD - 1 if side == 0 else PAD + ny
                for k, p in enumerate(CROSSING[2 + side]):
                    field[p, x + 1, row : row + 1, :] = y_recv[step, side, k, pl.ds(x, 1), :]
            return carry

        lax.fori_loop(0, nx, unpack, 0)

    def begin(x):
        for start in range(0, ny, BS):
            values = [pop_ref[p, x, start : start + BS, :].astype(jnp.float32) for p in range(POPS)]
            put(first, x, start, BS, collide(values, rate_ref[start : start + BS, :]))

    def middle(x, starts):
        for start in starts:
            values = gather(first, x, start, 8)
            put(second, x, start, 8, collide(values, rate_ref[start : start + 8, :]))

    def finish(x):
        for start in range(0, ny, BS):
            values = gather(second, x, start, BS)
            for p in range(POPS):
                out_ref[p, x, start : start + BS, :] = values[p].astype(jnp.bfloat16)

    def sweep(low, high, work):
        def one(x, carry):
            work(x)
            return carry

        lax.fori_loop(low, high, one, 0)

    inner = range(8, ny - 8, 8)
    outer = (0, ny - 8)
    sweep(0, 2, lambda i: begin(i * (nx - 1)))
    x_copies = send_x(0, first)
    sweep(1, nx - 1, begin)
    y_copies = send_y(0, first)
    take_x(0, first, x_copies)
    sweep(0, nx, lambda x: middle(x, inner))
    take_y(0, first, y_copies)
    sweep(0, 2, lambda i: middle(i * (nx - 1), outer))
    x_copies = send_x(1, second)
    sweep(1, nx - 1, lambda x: middle(x, outer))
    y_copies = send_y(1, second)
    take_x(1, second, x_copies)
    take_y(1, second, y_copies)
    sweep(0, nx, finish)


def run_steps(populations, rates):
    _, nx, ny, nz = populations.shape
    field = pltpu.VMEM((POPS, nx + 2, ny + 2 * PAD, nz), jnp.float32)
    x_face = pltpu.VMEM((2, 2, 5, ny, nz), jnp.float32)
    y_face = pltpu.VMEM((2, 2, 5, nx, nz), jnp.float32)
    corner = pltpu.VMEM((2, 4, PAD, nz), jnp.float32)
    return pl.pallas_call(
        functools.partial(steps_kernel, nx, ny),
        out_shape=jax.ShapeDtypeStruct(populations.shape, jnp.bfloat16),
        in_specs=[pl.BlockSpec(memory_space=pltpu.VMEM)] * 2,
        out_specs=pl.BlockSpec(memory_space=pltpu.VMEM),
        scratch_shapes=[
            field,
            field,
            x_face,
            x_face,
            y_face,
            y_face,
            corner,
            corner,
            pltpu.SemaphoreType.DMA((2, len(NEIGHBOURS))),
            pltpu.SemaphoreType.DMA((2, len(NEIGHBOURS))),
        ],
        compiler_params=pltpu.CompilerParams(
            collective_id=0, has_side_effects=True, vmem_limit_bytes=48 * 2**20
        ),
        name="steps",
    )(populations, rates)


ROWS = 32
CHUNK = 4


def layout_kernel(nx, ny, nz, state_ref, select_ref, pool_ref, fine, packed):
    eighths = ny // 8
    across = nz // BS
    fine[...] = jnp.zeros_like(fine)

    def part(c, carry):
        for inner in range(CHUNK):
            x = c * CHUNK + inner
            for p in range(POPS):
                fine[p * ny : (p + 1) * ny, :] = state_ref[p, x].astype(jnp.float32)
            for e in range(eighths):
                row = (inner * eighths + e) * ROWS
                for j in range(8):
                    rows = fine[pl.ds(e * 8 + j, ROWS, stride=ny), :]
                    packed[row : row + ROWS, j * nz : (j + 1) * nz] = rows.astype(jnp.bfloat16)
        result = jnp.dot(packed[...], select_ref[...], preferred_element_type=jnp.float32)
        result = result.astype(jnp.bfloat16)
        for inner in range(CHUNK):
            for e in range(eighths):
                row = (inner * eighths + e) * ROWS
                lanes = pl.ds(pl.multiple_of((c * CHUNK * 2 + inner * 2 + e % 2) * 128, 128), 128)
                for k in range(across):
                    pool_ref[e // 2 * across + k, :, lanes] = result[
                        row : row + POPS, k * 128 : (k + 1) * 128
                    ]
        return carry

    lax.fori_loop(0, nx // CHUNK, part, 0)


def lay_out(state):
    _, nx, ny, nz = state.shape
    across = nz // BS
    select = np.zeros((8 * nz, across * 128), np.float32)
    for j in range(8):
        for z in range(nz):
            select[j * nz + z, z // BS * 128 + j * BS + z % BS] = 1.0
    blocks = ny // BS * across
    return pl.pallas_call(
        functools.partial(layout_kernel, nx, ny, nz),
        out_shape=jax.ShapeDtypeStruct((blocks, POPS, BS**3), jnp.bfloat16),
        in_specs=[pl.BlockSpec(memory_space=pltpu.VMEM)] * 2,
        out_specs=pl.BlockSpec(memory_space=pltpu.VMEM),
        scratch_shapes=[
            pltpu.VMEM((ROWS * ny, nz), jnp.float32),
            pltpu.VMEM((CHUNK * (ny // 8) * ROWS, 8 * nz), jnp.bfloat16),
        ],
        compiler_params=pltpu.CompilerParams(vmem_limit_bytes=32 * 2**20),
        cost_estimate=pl.CostEstimate(
            flops=2 * state.size * across * 128, bytes_accessed=8 * state.size, transcendentals=0
        ),
        name="layout",
    )(state, jnp.asarray(select, jnp.bfloat16))


LANES = BS**3 // 128
QUADS = HALF // 2


def merge_kernel(nx, ny, leaving_ref, state_ref, shrink_ref, select_ref, out_ref, fine, packed, held):
    nz = state_ref.shape[3]
    rows = ny // BS
    across = nz // BS
    groups = nx // 4
    fine[...] = jnp.zeros_like(fine)
    for p in range(POPS):
        planes = [
            jnp.concatenate([state_ref[p, g * 4 + i] for i in range(4)], axis=1)
            for g in range(groups)
        ]
        fine[p * groups * ny : (p + 1) * groups * ny, :] = jnp.dot(
            jnp.concatenate(planes, axis=0), shrink_ref[...], preferred_element_type=jnp.float32
        )
    for g in range(groups):
        for r in range(rows):
            row = (g * rows + r) * ROWS
            for j in range(HALF):
                start = g * ny + r * BS + 2 * j
                value = (
                    fine[pl.ds(start, ROWS, stride=groups * ny), :]
                    + fine[pl.ds(start + 1, ROWS, stride=groups * ny), :]
                )
                packed[row : row + ROWS, j * 128 : (j + 1) * 128] = value.astype(jnp.bfloat16)
    result = jnp.dot(packed[...], select_ref[...], preferred_element_type=jnp.float32)
    result = result.astype(jnp.bfloat16)
    for g in range(groups):
        for r in range(rows):
            row = (g * rows + r) * ROWS
            for k in range(across):
                held[r * across + k, :, g * 128 : (g + 1) * 128] = result[
                    row : row + POPS, k * 128 : (k + 1) * 128
                ]

    def give(target, carry):
        out_ref[target] = held[leaving_ref[target]]
        return carry

    lax.fori_loop(0, out_ref.shape[0], give, 0)


def merge(leaving, state):
    _, nx, ny, nz = state.shape
    across = nz // BS
    shrink = np.zeros((4, nz, 2, across, HALF), np.float32)
    for i in range(4):
        for z in range(nz):
            shrink[i, z, i // 2, z // BS, z % BS // 2] = 0.125
    shrink = shrink.reshape(4 * nz, 2 * across * HALF)
    select = np.zeros((HALF, 2, across, HALF, across, 2, HALF, HALF), np.float32)
    for j in range(HALF):
        for half in range(2):
            for k in range(across):
                for z in range(HALF):
                    select[j, half, k, z, k, half, j, z] = 1.0
    select = select.reshape(HALF * 2 * across * HALF, across * 128)
    blocks = ny // BS * across
    groups = nx // 4
    return pl.pallas_call(
        functools.partial(merge_kernel, nx, ny),
        out_shape=jax.ShapeDtypeStruct((leaving.shape[0], POPS, HALF**3), jnp.bfloat16),
        in_specs=[pl.BlockSpec(memory_space=pltpu.SMEM)]
        + [pl.BlockSpec(memory_space=pltpu.VMEM)] * 3,
        out_specs=pl.BlockSpec(memory_space=pltpu.VMEM),
        scratch_shapes=[
            pltpu.VMEM((ROWS * groups * ny, 128), jnp.float32),
            pltpu.VMEM((groups * (ny // BS) * ROWS, HALF * 128), jnp.bfloat16),
            pltpu.VMEM((blocks, POPS, HALF**3), jnp.bfloat16),
        ],
        compiler_params=pltpu.CompilerParams(vmem_limit_bytes=32 * 2**20),
        name="merge",
    )(leaving, state, jnp.asarray(shrink, jnp.bfloat16), jnp.asarray(select, jnp.bfloat16))


def fill_kernel(
    source_ref,
    origin_ref,
    kind_ref,
    pool_source,
    incoming_ref,
    spread_ref,
    out_ref,
    held,
    packed,
    wide,
    pool_ref,
    pool_sem,
):
    fetch = pltpu.make_async_copy(pool_source, pool_ref, pool_sem)
    fetch.start()
    blocks = pool_ref.shape[0]
    arrivals = origin_ref.shape[0]
    packed[...] = jnp.zeros_like(packed)

    def load(a, carry):
        kind = kind_ref[a]
        value = incoming_ref[origin_ref[a]]
        zero = jnp.zeros_like(value)
        for half in range(2):
            part = jnp.where(kind == half + 1, value, zero)
            for q in range(QUADS):
                packed[a * QUADS + q, 0:POPS, half * 128 : (half + 1) * 128] = part[
                    :, q * 128 : (q + 1) * 128
                ]
        return carry

    lax.fori_loop(0, arrivals, load, 0)

    def expand(a, carry):
        rows = packed[pl.ds(a * 4 * QUADS, 4 * QUADS)].reshape(4 * QUADS * ROWS, 256)
        product = jnp.dot(rows, spread_ref[...], preferred_element_type=jnp.float32)
        wide[pl.ds(a * 4 * QUADS, 4 * QUADS)] = product.reshape(4 * QUADS, ROWS, 4 * 128)
        return carry

    lax.fori_loop(0, arrivals // 4, expand, 0)
    fetch.wait()

    def place(slot, carry):
        source = source_ref[slot]
        rows = pl.ds(slot, POPS, stride=CAP)

        @pl.when(source < blocks)
        def _():
            value = pool_ref[jnp.minimum(source, blocks - 1)].astype(jnp.float32)
            for k in range(LANES):
                held[k, rows, :] = value[:, k * 128 : (k + 1) * 128]

        @pl.when((source >= blocks) & (source < blocks + arrivals))
        def _():
            index = jnp.clip(source - blocks, 0, arrivals - 1)
            linear = kind_ref[index] == 2
            near = jnp.where(linear, 0.75, 1.0)
            far = jnp.where(linear, 0.25, 0.0)
            for part in range(2):
                slabs = []
                for h in range(HALF):
                    lane = h % 2 * 256 + part * 128
                    slabs.append(wide[index * QUADS + h // 2, 0:POPS, lane : lane + 128])
                for x in range(BS):
                    h = x // 2
                    other = max(h - 1, 0) if x % 2 == 0 else min(h + 1, HALF - 1)
                    held[x * 2 + part, rows, :] = near * slabs[h] + far * slabs[other]

        @pl.when(source >= blocks + arrivals)
        def _():
            for k in range(LANES):
                held[k, rows, :] = jnp.zeros((POPS, 128), jnp.float32)

        return carry

    lax.fori_loop(0, CAP, place, 0)

    def emit(p, carry):
        rows = pl.ds(pl.multiple_of(p * CAP, 8), CAP)
        for k in range(LANES):
            out_ref[p, :, k * 128 : (k + 1) * 128] = held[k, rows, :].astype(jnp.bfloat16)
        return carry

    lax.fori_loop(0, POPS, emit, 0)


def fill(source, origin, kinds, pool, incoming):
    parent = np.arange(BS) // 2
    step = np.where(np.arange(BS) % 2 == 0, -1, 1)
    neighbour = np.clip(parent + step, 0, HALF - 1)
    inject = (parent[:, None] == np.arange(HALF)[None, :]).astype(np.float32)
    linear = 0.75 * inject + 0.25 * (neighbour[:, None] == np.arange(HALF)[None, :])
    spread = np.concatenate(
        [np.kron(np.eye(2), np.kron(matrix, matrix).T) for matrix in (inject, linear)], axis=0
    )
    count = origin.shape[0]
    slotted = pl.pallas_call(
        fill_kernel,
        out_shape=jax.ShapeDtypeStruct((POPS, CAP, BS**3), jnp.bfloat16),
        in_specs=[pl.BlockSpec(memory_space=pltpu.SMEM)] * 3
        + [pl.BlockSpec(memory_space=pl.ANY)]
        + [pl.BlockSpec(memory_space=pltpu.VMEM)] * 2,
        out_specs=pl.BlockSpec(memory_space=pltpu.VMEM),
        scratch_shapes=[
            pltpu.VMEM((LANES, POPS * CAP, 128), jnp.float32),
            pltpu.VMEM((count * QUADS, ROWS, 256), jnp.bfloat16),
            pltpu.VMEM((count * QUADS, ROWS, 512), jnp.float32),
            pltpu.VMEM(pool.shape, jnp.bfloat16),
            pltpu.SemaphoreType.DMA(()),
        ],
        compiler_params=pltpu.CompilerParams(vmem_limit_bytes=61 * 2**20),
        name="fill",
    )(source, origin, kinds, pool, incoming, jnp.asarray(spread, jnp.bfloat16))
    return jnp.transpose(slotted, (1, 0, 2))


def body(populations, levels, refine_flags, new_owner):
    slab_count = lax.axis_size("gx")
    column_count = lax.axis_size("yz")
    slab = lax.axis_index("gx")
    column = lax.axis_index("yz")
    me = slab * column_count + column
    devices = slab_count * column_count
    _, nx, ny, nz = populations.shape
    across = nz // BS
    rows = ny // BS
    local = rows * across
    base = me * local
    block_total = new_owner.shape[0]

    local_levels = lax.dynamic_slice(levels, (base,), (local,)).reshape(rows, across)
    block_rates = 1.0 / (0.5 + jnp.power(0.5, local_levels.astype(jnp.float32)))
    rates = jnp.repeat(jnp.repeat(block_rates, BS, 0), BS, 1)

    ids = jnp.arange(block_total, dtype=jnp.int32)
    owned = new_owner == me
    before = owned[None, :] & (ids[None, :] < ids[:, None])
    rank = jnp.sum(before.astype(jnp.int32), axis=1)
    slots = jnp.arange(CAP, dtype=jnp.int32)
    hit = owned[None, :] & (rank[None, :] == slots[:, None])
    slot_id = jnp.sum(jnp.where(hit, ids[None, :], 0), axis=1)
    slot_kind = jnp.sum(jnp.where(hit, refine_flags[None, :], 0), axis=1)
    slot_used = jnp.any(hit, axis=1)
    flagged = slot_kind != 0
    slot_rank = jnp.sum(
        (flagged[None, :] & (slots[None, :] < slots[:, None])).astype(jnp.int32), axis=1
    )
    order = jnp.arange(2 * MIG, dtype=jnp.int32)
    match = flagged[None, :] & (slot_rank[None, :] == order[:, None])
    arrival_id = jnp.sum(jnp.where(match, slot_id[None, :], 0), axis=1)
    arrival_kind = jnp.sum(jnp.where(match, slot_kind[None, :], 0), axis=1)
    source = jnp.where(
        slot_used,
        jnp.where(flagged, local + slot_rank, slot_id % local),
        local + 2 * MIG,
    )

    local_flags = lax.dynamic_slice(refine_flags, (base,), (local,))
    local_owner = lax.dynamic_slice(new_owner, (base,), (local,))
    leaving = (local_flags != 0)[None, :] & (
        local_owner[None, :] == jnp.arange(devices, dtype=jnp.int32)[:, None]
    )
    leaving_block = jnp.sum(
        jnp.where(leaving, jnp.arange(local, dtype=jnp.int32)[None, :], 0), axis=1
    )

    state = run_steps(populations, rates)
    outgoing = merge(leaving_block, state)
    incoming = lax.all_to_all(outgoing, ("gx", "yz"), split_axis=0, concat_axis=0, tiled=True)
    pool = lay_out(state)
    return fill(source, arrival_id // local, arrival_kind, pool, incoming)


def solution(mesh):
    placed = (P(None, "gx", "yz", None), P(), P(), P())
    return jax.shard_map(
        body, mesh=mesh, in_specs=placed, out_specs=P(("gx", "yz"), None, None), check_vma=False
    )
```
